32 devices in a mesh: src: 4 (over z), rcv: 8 (over y, x, core).
Axes of the slice: x: 2, y: 2, z: 4, core: 2. Of those that a mesh axis runs over, the one named last changes fastest.
Arguments:
- records: bfloat16 [512, 512, 512], P('src', 'rcv'), may hold values from -6 to 6
- surface_operator: float32 [256, 2], replicated, may hold values from -0.7 to 0.7
Outputs:
- multiples: bfloat16 [512, 512, 512], P('src', 'rcv')
The draws below stay inside these ranges and needn't reach their ends.
All inputs are finite; a program needn't handle non-finite values.
Results may differ from the reference program's by a relative error of at most 0.011.
Values may be sent and summed in bfloat16 or wider, within the bound.
No kernel may reach another device: no remote copies, remote signals or barrier semaphores. Data moves between devices by JAX's collectives and lax.ppermute only.
A program may use at most 128 MiB of HBM per device.

```python
import math
import jax
import jax.numpy as jnp
from jax import lax

NS = 512
NT = 512
NF = 256


def block_scale(own_key, shape, cuts, low, high):
    def one(dim, shards_of):
        steps = jax.random.uniform(jax.random.fold_in(jax.random.fold_in(own_key, 6), dim), (shards_of,), jnp.float32, low / len(cuts), high / len(cuts))
        return jnp.repeat(jnp.exp(steps), shape[dim] // shards_of).reshape((-1,) + (1,) * (len(shape) - dim - 1))

    level = one(*cuts[0])
    for cut in cuts[1:]:
        level = level * one(*cut)
    return level


def centred(key, extent, spread, limit, split=(), dtype=jnp.bfloat16):
    drawn = spread * jax.random.normal(key, extent, jnp.float32)
    if split:
        drawn = drawn * block_scale(key, extent, split, -0.22, 0.18)
    return jnp.clip(drawn, -limit, limit).astype(dtype)


def setup_inputs(seed: int = 0) -> dict:
    splits = jax.random.split(jax.random.key(seed), 3)
    return {
        "records": centred(splits[0], (NS, NS, NT), 1.0, 6.0, ((0, 4), (1, 8))),
        "surface_operator": jnp.clip(jax.random.uniform(splits[1], (NF, 2), jnp.float32, -0.7, 0.7), -0.7, 0.7),
    }


def dft_tables(freqs, samples):
    freq_index = lax.broadcasted_iota(jnp.int32, (freqs, samples), 0)
    time_index = lax.broadcasted_iota(jnp.int32, (freqs, samples), 1)
    phase = (freq_index * time_index % samples).astype(jnp.float32)
    angle = phase * (2.0 * math.pi / samples)
    norming = 1.0 / math.sqrt(samples)
    cosine = jnp.cos(angle) * norming
    sine = jnp.sin(angle) * norming
    weights = jnp.where(freq_index == 0, 1.0, 2.0).astype(jnp.float32)
    forward = jnp.stack([cosine, -sine], axis=1).reshape(2 * freqs, samples)
    inverse = jnp.stack([weights * cosine, -weights * sine], axis=1).reshape(2 * freqs, samples)
    return (forward.astype(jnp.bfloat16), inverse.astype(jnp.bfloat16))

def complex_product(left, right):
    real_part = jnp.dot(left[0], right[0], preferred_element_type=jnp.float32) - jnp.dot(left[1], right[1], preferred_element_type=jnp.float32)
    imag_part = jnp.dot(left[0], right[1], preferred_element_type=jnp.float32) + jnp.dot(left[1], right[0], preferred_element_type=jnp.float32)
    return (real_part, imag_part)

def predict_one(block, coeff):
    recip = (0.5 * (block.astype(jnp.float32) + jnp.swapaxes(block, 1, 2).astype(jnp.float32))).astype(jnp.bfloat16)
    factor = coeff / math.sqrt(NS)

    def scaled(product):
        return jnp.stack([factor[0] * product[0] - factor[1] * product[1], factor[0] * product[1] + factor[1] * product[0]])
    first = scaled(complex_product(recip, recip)).astype(jnp.bfloat16)
    second = scaled(complex_product(recip, first)).astype(jnp.bfloat16)
    third = scaled(complex_product(recip, second))
    return (first.astype(jnp.float32) + second.astype(jnp.float32) + third).astype(jnp.bfloat16)

def reference(records, surface_operator):
    forward, inverse = dft_tables(NF, NT)
    flat_traces = records.reshape(NS * NS, NT)
    spectrum = jnp.dot(forward, flat_traces.T, preferred_element_type=jnp.float32).astype(jnp.bfloat16)
    spectrum = spectrum.reshape(NF, 2, NS, NS)

    def per_freq(pair):
        return predict_one(pair[0], pair[1])
    predicted = lax.map(per_freq, (spectrum, surface_operator))
    result = jnp.dot(predicted.reshape(2 * NF, NS * NS).T, inverse, preferred_element_type=jnp.float32)
    return result.astype(jnp.bfloat16).reshape(NS, NS, NT)
```

```python
import math

import jax
import jax.numpy as jnp
from jax import lax
from jax.sharding import PartitionSpec as P
from jax.experimental import pallas as pl
from jax.experimental.pallas import tpu as pltpu
import ml_dtypes
import numpy as np


def dft_tables(freqs, samples):
    freq_index = lax.broadcasted_iota(jnp.int32, (freqs, samples), 0)
    time_index = lax.broadcasted_iota(jnp.int32, (freqs, samples), 1)
    phase = (freq_index * time_index % samples).astype(jnp.float32)
    angle = phase * (2.0 * math.pi / samples)
    norming = 1.0 / math.sqrt(samples)
    cosine = jnp.cos(angle) * norming
    sine = jnp.sin(angle) * norming
    weights = jnp.where(freq_index == 0, 1.0, 2.0).astype(jnp.float32)
    forward = jnp.stack([cosine, -sine], axis=1).reshape(2 * freqs, samples)
    inverse = jnp.stack([weights * cosine, -weights * sine], axis=1).reshape(2 * freqs, samples)
    return (forward.astype(jnp.bfloat16), inverse.astype(jnp.bfloat16))


def batch_product(left, right):

    def mult(first_op, second_op):
        return jnp.einsum("nij,njk->nik", first_op, second_op, preferred_element_type=jnp.float32)

    real_part = mult(left[:, 0], right[:, 0]) - mult(left[:, 1], right[:, 1])
    imag_part = mult(left[:, 0], right[:, 1]) + mult(left[:, 1], right[:, 0])
    return (real_part, imag_part)


def predict_block(blocks, coeff):
    order = blocks.shape[2]
    recip = (
        0.5 * (blocks.astype(jnp.float32) + jnp.swapaxes(blocks, 2, 3).astype(jnp.float32))
    ).astype(jnp.bfloat16)
    factor = coeff / math.sqrt(order)
    real_k = factor[:, 0][:, None, None]
    imag_k = factor[:, 1][:, None, None]

    def scaled(product):
        return jnp.stack(
            [real_k * product[0] - imag_k * product[1], real_k * product[1] + imag_k * product[0]],
            axis=1,
        )

    first = scaled(batch_product(recip, recip)).astype(jnp.bfloat16)
    second = scaled(batch_product(recip, first)).astype(jnp.bfloat16)
    third = scaled(batch_product(recip, second))
    return (first.astype(jnp.float32) + second.astype(jnp.float32) + third).astype(jnp.bfloat16)


def local_general(records, surface_operator):
    src_tiles, rcv_tiles, samples = records.shape
    freqs = surface_operator.shape[0]
    n_src = lax.axis_size("src")
    n_rcv = lax.axis_size("rcv")
    per_group = freqs // (n_src * n_rcv)
    columns = src_tiles * rcv_tiles
    whole_src = n_src * src_tiles
    whole_rcv = n_rcv * rcv_tiles
    forward, inverse = dft_tables(freqs, samples)
    flat_traces = records.reshape(columns, samples)
    spectrum = jnp.einsum(
        "kt,nt->kn", forward, flat_traces, preferred_element_type=jnp.float32
    ).astype(jnp.bfloat16)
    group_index = lax.axis_index("src") * n_rcv + lax.axis_index("rcv")
    coeff = lax.dynamic_slice_in_dim(surface_operator, group_index * per_group, per_group, 0)
    moved = lax.all_to_all(
        spectrum.reshape(freqs, 2, 1, columns),
        ("src", "rcv"),
        split_axis=0,
        concat_axis=2,
        tiled=True,
    )
    blocks = moved.reshape(per_group, 2, n_src, n_rcv, src_tiles, rcv_tiles)
    blocks = blocks.transpose(0, 1, 2, 4, 3, 5).reshape(per_group, 2, whole_src, whole_rcv)
    predicted = predict_block(blocks, coeff)
    outgoing = predicted.reshape(per_group, 2, n_src, src_tiles, n_rcv, rcv_tiles).transpose(
        0, 1, 2, 4, 3, 5
    )
    returned = lax.all_to_all(
        outgoing.reshape(1, per_group, 2, n_src * n_rcv, columns),
        ("src", "rcv"),
        split_axis=3,
        concat_axis=0,
        tiled=True,
    )
    returned = returned.reshape(2 * freqs, columns)
    result = jnp.einsum("kn,kt->nt", returned, inverse, preferred_element_type=jnp.float32)
    return result.astype(jnp.bfloat16).reshape(src_tiles, rcv_tiles, samples)


NT = (((1,), (1,)), ((), ()))
TN = (((0,), (0,)), ((), ()))
VMEM_LIMIT = 56 * 2**20
ROWS = 16


def host_tables(freqs, samples):
    f = np.arange(freqs)[:, None]
    t = np.arange(samples)[None, :]
    angle = (f * t % samples) * (2.0 * math.pi / samples)
    norming = 1.0 / math.sqrt(samples)
    cosine = np.cos(angle) * norming
    sine = np.sin(angle) * norming
    weights = np.where(f == 0, 1.0, 2.0)
    forward = np.stack([cosine, -sine], axis=1)
    inverse = np.stack([weights * cosine, -weights * sine], axis=1)
    to = lambda x: x.astype(np.float32).astype(ml_dtypes.bfloat16).reshape(2 * freqs, samples)
    return to(forward), to(inverse)


def forward_dft(records, table):
    sources, receivers, samples = records.shape
    half = sources // 2
    width = 2 * receivers
    rows = table.shape[0]

    def kernel(table_ref, records_ref, out_ref, turned):
        for p in range(0, ROWS, 2):
            traces = jnp.concatenate(
                [records_ref[s, p + d] for d in range(2) for s in range(2)], axis=0
            )
            found = lax.dot_general(
                table_ref[...], traces, NT, preferred_element_type=jnp.float32
            )
            turned[p] = found[:, :width]
            turned[p + 1] = found[:, width:]
        out_ref[...] = jnp.swapaxes(turned[...], 0, 1).astype(out_ref.dtype)

    return pl.pallas_call(
        kernel,
        grid=(half // ROWS,),
        in_specs=[
            pl.BlockSpec((rows, samples), lambda i: (0, 0)),
            pl.BlockSpec((2, ROWS, receivers, samples), lambda i: (0, i, 0, 0)),
        ],
        out_specs=pl.BlockSpec((rows, ROWS, width), lambda i: (0, i, 0)),
        out_shape=jax.ShapeDtypeStruct((rows, half, width), jnp.bfloat16),
        scratch_shapes=[pltpu.VMEM((ROWS, rows, width), jnp.float32)],
        compiler_params=pltpu.CompilerParams(vmem_limit_bytes=VMEM_LIMIT),
        cost_estimate=pl.CostEstimate(
            flops=2 * rows * records.size,
            bytes_accessed=2 * (records.size + rows * half * width),
            transcendentals=0,
        ),
    )(table, records.reshape(2, half, receivers, samples))


def inverse_dft(spectra, table):
    rows, half, width = spectra.shape
    receivers = width // 2
    samples = table.shape[1]

    def kernel(table_ref, spectra_ref, out_ref, turned):
        turned[...] = jnp.swapaxes(spectra_ref[...].astype(jnp.float32), 0, 1)
        for p in range(ROWS):
            traces = lax.dot_general(
                turned[p].astype(jnp.bfloat16),
                table_ref[...],
                TN,
                preferred_element_type=jnp.float32,
            ).astype(out_ref.dtype)
            out_ref[0, p] = traces[:receivers]
            out_ref[1, p] = traces[receivers:]

    return pl.pallas_call(
        kernel,
        grid=(half // ROWS,),
        in_specs=[
            pl.BlockSpec((rows, samples), lambda i: (0, 0)),
            pl.BlockSpec((rows, ROWS, width), lambda i: (0, i, 0)),
        ],
        out_specs=pl.BlockSpec((2, ROWS, receivers, samples), lambda i: (0, i, 0, 0)),
        out_shape=jax.ShapeDtypeStruct((2, half, receivers, samples), jnp.bfloat16),
        scratch_shapes=[pltpu.VMEM((ROWS, rows, width), jnp.float32)],
        compiler_params=pltpu.CompilerParams(vmem_limit_bytes=VMEM_LIMIT),
        cost_estimate=pl.CostEstimate(
            flops=2 * rows * half * width * samples,
            bytes_accessed=2 * (half * width * samples + rows * half * width),
            transcendentals=0,
        ),
    )(table, spectra).reshape(2 * half, receivers, samples)


def swap_quarters(block):
    size = block.shape[0]
    half = size // 2
    rolled = pltpu.roll(block, half, 1)
    left = lax.broadcasted_iota(jnp.int32, (half, size), 1) < half
    return jnp.concatenate(
        [
            jnp.where(left, block[:half], rolled[half:]),
            jnp.where(left, rolled[:half], block[half:]),
        ],
        axis=0,
    )


def dot(left, right):
    return jnp.dot(left, right, preferred_element_type=jnp.float32)


def series(coeff_ref, index, recip, first, out_block):
    order = recip.shape[-1]
    real_k = coeff_ref[index, 0]
    imag_k = coeff_ref[index, 1]
    panel = min(256, order)
    wide = jnp.float32

    def scaled(real, imag):
        return real_k * real - imag_k * imag, real_k * imag + imag_k * real

    for start in range(0, order, panel):
        rows = pl.ds(start, panel)
        a, b = recip[0, rows, :], recip[1, rows, :]
        real, imag = scaled(
            dot(a, recip[0]) - dot(b, recip[1]), dot(a, recip[1]) + dot(b, recip[0])
        )
        first[0, rows, :] = real.astype(jnp.bfloat16)
        first[1, rows, :] = imag.astype(jnp.bfloat16)
    for start in range(0, order, panel):
        rows = pl.ds(start, panel)
        own = [first[c, rows, :].astype(wide) for c in range(2)]
        a, b = [(recip[c, rows, :].astype(wide) + own[c]).astype(jnp.bfloat16) for c in range(2)]
        real, imag = scaled(
            dot(a, first[0]) - dot(b, first[1]), dot(a, first[1]) + dot(b, first[0])
        )
        out_block(start, panel, own[0] + real, own[1] + imag)


def predict(moved, coeff):
    devices, freqs, _, half, tile = moved.shape
    order = math.isqrt(devices * half * tile)
    blocks = order // tile
    pieces = 2 * blocks

    def kernel(coeff_ref, moved_ref, out_ref, recip, first):
        for c in range(2):
            for a in range(blocks):
                for b in range(a + 1):

                    def stacked(i, j):
                        at = i * pieces + 2 * j
                        return jnp.concatenate(
                            [moved_ref[at, 0, c], moved_ref[at + 1, 0, c]], axis=0
                        ).astype(jnp.float32)

                    mean = 0.5 * (stacked(a, b) + stacked(b, a).T)
                    block = swap_quarters(mean)
                    recip[c, a * tile:(a + 1) * tile, b * tile:(b + 1) * tile] = block.astype(
                        jnp.bfloat16
                    )
                    if a != b:
                        recip[c, b * tile:(b + 1) * tile, a * tile:(a + 1) * tile] = (
                            block.T.astype(jnp.bfloat16)
                        )

        def out_block(start, panel, real, imag):
            for c, value in enumerate((real, imag)):
                for row in range(0, panel, tile):
                    a = (start + row) // tile
                    for b in range(blocks):
                        block = swap_quarters(
                            value[row:row + tile, b * tile:(b + 1) * tile]
                        ).astype(jnp.bfloat16)
                        at = a * pieces + 2 * b
                        out_ref[at, 0, c] = block[:half]
                        out_ref[at + 1, 0, c] = block[half:]

        series(coeff_ref, pl.program_id(0), recip, first, out_block)

    spec = pl.BlockSpec((devices, 1, 2, half, tile), lambda i: (0, i, 0, 0, 0))
    return pl.pallas_call(
        kernel,
        grid=(freqs,),
        in_specs=[pl.BlockSpec(memory_space=pltpu.SMEM), spec],
        out_specs=spec,
        out_shape=jax.ShapeDtypeStruct(moved.shape, jnp.bfloat16),
        scratch_shapes=[
            pltpu.VMEM((2, order, order), jnp.bfloat16),
            pltpu.VMEM((2, order, order), jnp.bfloat16),
        ],
        compiler_params=pltpu.CompilerParams(vmem_limit_bytes=VMEM_LIMIT),
        cost_estimate=pl.CostEstimate(
            flops=16 * freqs * order**3, bytes_accessed=4 * moved.size, transcendentals=0
        ),
    )(coeff / math.sqrt(order), moved)


def local_tiles(records, surface_operator):
    src_tiles, rcv_tiles, samples = records.shape
    freqs = surface_operator.shape[0]
    axes = ("src", "rcv")
    n_src = lax.axis_size("src")
    n_rcv = lax.axis_size("rcv")
    devices = n_src * n_rcv
    per_group = freqs // devices
    half = src_tiles // 2
    forward, inverse = host_tables(freqs, samples)
    group_index = lax.axis_index("src") * n_rcv + lax.axis_index("rcv")
    coeff = lax.dynamic_slice_in_dim(surface_operator, group_index * per_group, per_group, 0)
    spectrum = forward_dft(records, jnp.asarray(forward))
    spectrum = spectrum.reshape(devices, per_group, 2, half, src_tiles)
    moved = lax.all_to_all(spectrum, axes, split_axis=0, concat_axis=0, tiled=True)
    predicted = predict(moved, coeff)
    returned = lax.all_to_all(predicted, axes, split_axis=0, concat_axis=0, tiled=True)
    return inverse_dft(returned.reshape(2 * freqs, half, src_tiles), jnp.asarray(inverse))


def solution(mesh):
    placed = (P("src", "rcv", None), P())
    n_src, n_rcv = mesh.shape["src"], mesh.shape["rcv"]

    def local(records, surface_operator):
        src_tiles, rcv_tiles, _ = records.shape
        whole_lanes = src_tiles % 128 == 0 and rcv_tiles % 32 == 0
        if n_rcv == 2 * n_src and src_tiles == 2 * rcv_tiles and whole_lanes:
            return local_tiles(records, surface_operator)
        return local_general(records, surface_operator)

    return jax.shard_map(
        local, mesh=mesh, in_specs=placed, out_specs=P("src", "rcv", None), check_vma=False
    )
```

```python
import math

import jax
import jax.numpy as jnp
from jax import lax
from jax.sharding import PartitionSpec as P
from jax.experimental import pallas as pl
from jax.experimental.pallas import tpu as pltpu
import ml_dtypes
import numpy as np


def dft_tables(freqs, samples):
    freq_index = lax.broadcasted_iota(jnp.int32, (freqs, samples), 0)
    time_index = lax.broadcasted_iota(jnp.int32, (freqs, samples), 1)
    phase = (freq_index * time_index % samples).astype(jnp.float32)
    angle = phase * (2.0 * math.pi / samples)
    norming = 1.0 / math.sqrt(samples)
    cosine = jnp.cos(angle) * norming
    sine = jnp.sin(angle) * norming
    weights = jnp.where(freq_index == 0, 1.0, 2.0).astype(jnp.float32)
    forward = jnp.stack([cosine, -sine], axis=1).reshape(2 * freqs, samples)
    inverse = jnp.stack([weights * cosine, -weights * sine], axis=1).reshape(2 * freqs, samples)
    return (forward.astype(jnp.bfloat16), inverse.astype(jnp.bfloat16))


def batch_product(left, right):

    def mult(first_op, second_op):
        return jnp.einsum("nij,njk->nik", first_op, second_op, preferred_element_type=jnp.float32)

    real_part = mult(left[:, 0], right[:, 0]) - mult(left[:, 1], right[:, 1])
    imag_part = mult(left[:, 0], right[:, 1]) + mult(left[:, 1], right[:, 0])
    return (real_part, imag_part)


def predict_block(blocks, coeff):
    order = blocks.shape[2]
    recip = (
        0.5 * (blocks.astype(jnp.float32) + jnp.swapaxes(blocks, 2, 3).astype(jnp.float32))
    ).astype(jnp.bfloat16)
    factor = coeff / math.sqrt(order)
    real_k = factor[:, 0][:, None, None]
    imag_k = factor[:, 1][:, None, None]

    def scaled(product):
        return jnp.stack(
            [real_k * product[0] - imag_k * product[1], real_k * product[1] + imag_k * product[0]],
            axis=1,
        )

    first = scaled(batch_product(recip, recip)).astype(jnp.bfloat16)
    second = scaled(batch_product(recip, first)).astype(jnp.bfloat16)
    third = scaled(batch_product(recip, second))
    return (first.astype(jnp.float32) + second.astype(jnp.float32) + third).astype(jnp.bfloat16)


def local_general(records, surface_operator):
    src_tiles, rcv_tiles, samples = records.shape
    freqs = surface_operator.shape[0]
    n_src = lax.axis_size("src")
    n_rcv = lax.axis_size("rcv")
    per_group = freqs // (n_src * n_rcv)
    columns = src_tiles * rcv_tiles
    whole_src = n_src * src_tiles
    whole_rcv = n_rcv * rcv_tiles
    forward, inverse = dft_tables(freqs, samples)
    flat_traces = records.reshape(columns, samples)
    spectrum = jnp.einsum(
        "kt,nt->kn", forward, flat_traces, preferred_element_type=jnp.float32
    ).astype(jnp.bfloat16)
    group_index = lax.axis_index("src") * n_rcv + lax.axis_index("rcv")
    coeff = lax.dynamic_slice_in_dim(surface_operator, group_index * per_group, per_group, 0)
    moved = lax.all_to_all(
        spectrum.reshape(freqs, 2, 1, columns),
        ("src", "rcv"),
        split_axis=0,
        concat_axis=2,
        tiled=True,
    )
    blocks = moved.reshape(per_group, 2, n_src, n_rcv, src_tiles, rcv_tiles)
    blocks = blocks.transpose(0, 1, 2, 4, 3, 5).reshape(per_group, 2, whole_src, whole_rcv)
    predicted = predict_block(blocks, coeff)
    outgoing = predicted.reshape(per_group, 2, n_src, src_tiles, n_rcv, rcv_tiles).transpose(
        0, 1, 2, 4, 3, 5
    )
    returned = lax.all_to_all(
        outgoing.reshape(1, per_group, 2, n_src * n_rcv, columns),
        ("src", "rcv"),
        split_axis=3,
        concat_axis=0,
        tiled=True,
    )
    returned = returned.reshape(2 * freqs, columns)
    result = jnp.einsum("kn,kt->nt", returned, inverse, preferred_element_type=jnp.float32)
    return result.astype(jnp.bfloat16).reshape(src_tiles, rcv_tiles, samples)


NT = (((1,), (1,)), ((), ()))
TN = (((0,), (0,)), ((), ()))
VMEM_LIMIT = 56 * 2**20
ROWS = 16
WIDE = jnp.float32
NARROW = jnp.bfloat16
IN_VMEM = pl.BlockSpec(memory_space=pltpu.VMEM)
IN_SMEM = pl.BlockSpec(memory_space=pltpu.SMEM)
UNREAD = pl.BlockSpec(memory_space=pl.ANY)


def host_tables(freqs, samples):
    f = np.arange(freqs)[:, None]
    t = np.arange(samples)[None, :]
    angle = (f * t % samples) * (2.0 * math.pi / samples)
    norming = 1.0 / math.sqrt(samples)
    cosine = np.cos(angle) * norming
    sine = np.sin(angle) * norming
    weights = np.where(f == 0, 1.0, 2.0)
    forward = np.stack([cosine, -sine], axis=1)
    inverse = np.stack([weights * cosine, -weights * sine], axis=1)
    return [x.astype(np.float32).astype(ml_dtypes.bfloat16) for x in (forward, inverse)]


def params():
    return pltpu.CompilerParams(vmem_limit_bytes=VMEM_LIMIT)


def cost(flops, moved):
    return pl.CostEstimate(flops=0, bytes_accessed=0, transcendentals=0)


def shaped(*shape):
    return jax.ShapeDtypeStruct(shape, NARROW)


def forward_dft(place, records, tables, after):
    sources, receivers, samples = records.shape
    half = sources // 2
    width = 2 * receivers
    sizes = [table.shape[1] for table in tables for _ in range(table.shape[0])]
    rows = sum(sizes)

    def kernel(place_ref, after_ref, *refs):
        table_refs, records_ref = refs[:len(tables)], refs[len(tables)]
        out_refs, (turned, table) = refs[len(tables) + 1:-2], refs[-2:]

        @pl.when(pl.program_id(0) == 0)
        def _():
            at = 0
            for ref in table_refs:
                parts, size, _ = ref.shape
                for part in range(parts):
                    which = (place_ref[0] ^ part) if parts > 1 else 0
                    table[at:at + size, :] = ref[which]
                    at += size

        for p in range(0, ROWS, 2):
            traces = jnp.concatenate(
                [records_ref[s, p + d] for d in range(2) for s in range(2)], axis=0
            )
            found = lax.dot_general(table[...], traces, NT, preferred_element_type=WIDE)
            turned[p] = found[:, :width]
            turned[p + 1] = found[:, width:]
        at = 0
        for out_ref, size in zip(out_refs, sizes):
            out_ref[...] = jnp.swapaxes(turned[:, at:at + size, :], 0, 1).astype(NARROW)
            at += size

    return pl.pallas_call(
        kernel,
        grid=(half // ROWS,),
        in_specs=[IN_SMEM, UNREAD]
        + [pl.BlockSpec(table.shape, lambda i: (0, 0, 0)) for table in tables]
        + [pl.BlockSpec((2, ROWS, receivers, samples), lambda i: (0, i, 0, 0))],
        out_specs=[pl.BlockSpec((size, ROWS, width), lambda i: (0, i, 0)) for size in sizes],
        out_shape=[shaped(size, half, width) for size in sizes],
        scratch_shapes=[
            pltpu.VMEM((ROWS, rows, width), WIDE),
            pltpu.VMEM((rows, samples), NARROW),
        ],
        compiler_params=params(),
        cost_estimate=cost(2 * rows * records.size, 2 * (records.size + rows * half * width)),
    )(place, after, *tables, records.reshape(2, half, receivers, samples))


def inverse_dft(place, pieces, tables):
    half, width = pieces[0][0].shape[1:]
    receivers = width // 2
    samples = tables[0].shape[-1]
    spectra = [piece for group in pieces for piece in group]
    sizes = [piece.shape[0] for piece in spectra]
    rows = sum(sizes)

    def kernel(place_ref, *refs):
        table_refs = refs[:len(tables)]
        spectra_refs = refs[len(tables):len(tables) + len(spectra)]
        out_ref, turned, table = refs[len(tables) + len(spectra):]

        @pl.when(pl.program_id(0) == 0)
        def _():
            at = 0
            for table_ref, group in zip(table_refs, pieces):
                for part, piece in enumerate(group):
                    size = piece.shape[0]
                    which = (place_ref[0] ^ part) if len(group) > 1 else 0
                    table[at:at + size, :] = table_ref[which]
                    at += size

        at = 0
        for ref, size in zip(spectra_refs, sizes):
            turned[:, at:at + size, :] = jnp.swapaxes(ref[...].astype(WIDE), 0, 1)
            at += size
        for p in range(ROWS):
            traces = lax.dot_general(
                turned[p].astype(NARROW), table[...], TN, preferred_element_type=WIDE
            ).astype(out_ref.dtype)
            out_ref[0, p] = traces[:receivers]
            out_ref[1, p] = traces[receivers:]

    return pl.pallas_call(
        kernel,
        grid=(half // ROWS,),
        in_specs=[IN_SMEM]
        + [pl.BlockSpec(table.shape, lambda i: (0, 0, 0)) for table in tables]
        + [pl.BlockSpec((size, ROWS, width), lambda i: (0, i, 0)) for size in sizes],
        out_specs=pl.BlockSpec((2, ROWS, receivers, samples), lambda i: (0, i, 0, 0)),
        out_shape=shaped(2, half, receivers, samples),
        scratch_shapes=[
            pltpu.VMEM((ROWS, rows, width), WIDE),
            pltpu.VMEM((rows, samples), NARROW),
        ],
        compiler_params=params(),
        cost_estimate=cost(
            2 * rows * half * width * samples, 2 * half * width * (samples + rows)
        ),
    )(place, *tables, *spectra).reshape(2 * half, receivers, samples)


def swap_quarters(block):
    size = block.shape[0]
    half = size // 2
    rolled = pltpu.roll(block, half, 1)
    left = left_half(half, size)
    return jnp.concatenate(
        [
            jnp.where(left, block[:half], rolled[half:]),
            jnp.where(left, rolled[:half], block[half:]),
        ],
        axis=0,
    )


def left_half(rows, lanes):
    return lax.broadcasted_iota(jnp.int32, (rows, lanes), 1) < lanes // 2


def pack_diagonals(real, imag):
    half, size = real.shape[0] // 2, real.shape[0]
    last = jnp.where(left_half(half, size), pltpu.roll(real[half:], half, 1), imag[half:])
    return real[:half], imag[:half], last


def unpack_diagonal(top, last, c):
    half, size = top.shape
    if c == 0:
        last = pltpu.roll(last, half, 1)
    mirrored = jnp.concatenate([top, top], axis=0).T
    return jnp.concatenate([top, jnp.where(left_half(half, size), mirrored[half:], last)], axis=0)


def square(ref, *at):
    halves = ref[at] if at else ref[...]
    return halves.astype(WIDE).reshape(2 * halves.shape[-2], halves.shape[-1])


def dot(left, right):
    return jnp.dot(left, right, preferred_element_type=WIDE)


def series(real_k, imag_k, recip, first, out_block, tile):
    order = recip.shape[-1]
    panel = min(2 * tile, order)

    def scaled(real, imag):
        return real_k * real - imag_k * imag, real_k * imag + imag_k * real

    for start in range(0, order, panel):
        rows = pl.ds(start, panel)
        a, b = recip[0, rows, :], recip[1, rows, :]
        real, imag = scaled(
            dot(a, recip[0]) - dot(b, recip[1]), dot(a, recip[1]) + dot(b, recip[0])
        )
        first[0, rows, :] = real.astype(NARROW)
        first[1, rows, :] = imag.astype(NARROW)
    for start in range(0, order, panel):
        rows = pl.ds(start, panel)
        own = [first[c, rows, :].astype(WIDE) for c in range(2)]
        a, b = [(recip[c, rows, :].astype(WIDE) + own[c]).astype(NARROW) for c in range(2)]
        real, imag = scaled(
            dot(a, first[0]) - dot(b, first[1]), dot(a, first[1]) + dot(b, first[0])
        )
        real, imag = own[0] + real, own[1] + imag
        for row in range(0, panel, tile):
            for b in range(order // tile):
                at = (slice(row, row + tile), slice(b * tile, (b + 1) * tile))
                out_block(
                    (start + row) // tile, b, swap_quarters(real[at]), swap_quarters(imag[at])
                )


def far_units(n):
    pair = 4 * (n - 2)
    return pair, pair + 2, pair + 5


def predict(place, coeff, moved, n, direct_in, direct_out, start, stop, after):
    freqs = stop - start
    half, tile = moved[0].shape[-2:]
    order = n * tile
    pair_at, diagonal_at, units = far_units(n)

    def kernel(place_ref, coeff_ref, after_ref, *refs):
        count = 1 if direct_in else n
        moved_refs, refs = refs[:count], refs[count:]
        count = 1 if direct_out else n
        out_refs, (recip, first) = refs[:count], refs[count:]
        me = place_ref[0]
        odd = me % 2 == 1

        def stacked(c, i, j):
            if direct_in:
                return square(moved_refs[0], pl.ds((j ^ me) * 2, 2), i, 0, c)
            if i < 2:
                return square(moved_refs[i], i ^ j, 0, c)
            return square(moved_refs[i], 0, pl.ds(((i ^ j) - 2) * 4 + 2 * c, 2))

        def mean(c, a, b):
            if direct_in or a < 2 or (a ^ b) >= 2:
                return 0.5 * (stacked(c, a, b) + stacked(c, b, a).T)
            if a == b:
                ref = moved_refs[a]
                top = ref[0, diagonal_at + c].astype(WIDE)
                return unpack_diagonal(top, ref[0, diagonal_at + 2].astype(WIDE), c)
            here = square(moved_refs[a], 0, pl.ds(pair_at, 2))
            there = square(moved_refs[b], 0, pl.ds(pair_at, 2)).T
            return jnp.where(odd == (c == 0), here, there)

        for c in range(2):
            for a in range(n):
                for b in range(a + 1):
                    block = swap_quarters(mean(c, a, b))
                    rows, columns = slice(a * tile, (a + 1) * tile), slice(b * tile, (b + 1) * tile)
                    recip[c, rows, columns] = block.astype(NARROW)
                    if a != b:
                        recip[c, columns, rows] = block.T.astype(NARROW)

        def out_block(a, b, real, imag):
            gap = a ^ b
            if not direct_out and a >= 2 and gap == 1:
                own = jnp.where(odd == (a % 2 == 0), imag, real).astype(NARROW)
                out_refs[a][0, pair_at] = own[:half]
                out_refs[a][0, pair_at + 1] = own[half:]
                return
            if not direct_out and a >= 2 and gap == 0:
                for unit, value in enumerate(pack_diagonals(real, imag)):
                    out_refs[a][0, diagonal_at + unit] = value.astype(NARROW)
                return
            for c, value in enumerate((real, imag)):
                value = value.astype(NARROW)
                for h in range(2):
                    part = value[h * half:(h + 1) * half]
                    if direct_out:
                        out_refs[0][(b ^ me) * 2 + h, a, 0, c] = part
                    elif a < 2:
                        out_refs[a][gap, 0, c, h] = part
                    else:
                        out_refs[a][0, (gap - 2) * 4 + 2 * c + h] = part

        index = pl.program_id(0) + start
        series(coeff_ref[index, 0], coeff_ref[index, 1], recip, first, out_block, tile)

    whole = (2 * n, n, freqs, 2, half, tile)
    close = (n, freqs, 2, 2, half, tile)
    far = (freqs, units, half, tile)
    split_shapes = [shaped(*close)] * 2 + [shaped(*far)] * (n - 2)

    def specs(direct, first):
        if direct:
            block = (2 * n, n, 1, 2, half, tile)
            return [pl.BlockSpec(block, lambda i: (0, 0, i + first, 0, 0, 0))]
        close = pl.BlockSpec((n, 1, 2, 2, half, tile), lambda i: (0, i + first, 0, 0, 0, 0))
        far = pl.BlockSpec((1, units, half, tile), lambda i: (i + first, 0, 0, 0))
        return [close] * 2 + [far] * (n - 2)

    return pl.pallas_call(
        kernel,
        grid=(freqs,),
        in_specs=[IN_SMEM, IN_SMEM, UNREAD] + specs(direct_in, start),
        out_specs=specs(direct_out, 0),
        out_shape=[shaped(*whole)] if direct_out else split_shapes,
        scratch_shapes=[pltpu.VMEM((2, order, order), NARROW)] * 2,
        compiler_params=params(),
        cost_estimate=cost(16 * freqs * order**3, 16 * freqs * order**2),
    )(place, coeff / math.sqrt(order), after, *moved)


def gather_rows(place, moved, pairs, n, after):
    _, _, freqs, _, half, tile = moved.shape
    pair_at, diagonal_at, units = far_units(n)

    def kernel(place_ref, after_ref, moved_ref, pairs_ref, *out_refs):
        me = place_ref[0]
        mine = me % 2

        def halves(block):
            return pl.ds((me ^ block) * 2, 2)

        for d in range(2):
            for block in range(n):
                for f in range(freqs):
                    for c in range(2):
                        out_refs[d][block, f, c] = moved_ref[halves(block), me ^ d, f, c]
        for d in range(2, n):
            for f in range(freqs):
                for block in range(2, n):
                    for c in range(2):
                        at = (block - 2) * 4 + 2 * c
                        out_refs[d][f, at:at + 2] = moved_ref[halves(block), me ^ d, f, c]
                here = square(moved_ref, halves(1), me ^ d, f, mine)
                there = square(pairs_ref, (d ^ 1) - 2, slice(None), f)
                mean = (0.5 * (here + there.T)).astype(NARROW)
                out_refs[d][f, pair_at] = mean[:half]
                out_refs[d][f, pair_at + 1] = mean[half:]
                means = []
                for c in range(2):
                    block = square(moved_ref, halves(0), me ^ d, f, c)
                    means.append(0.5 * (block + block.T))
                for unit, value in enumerate(pack_diagonals(*means)):
                    out_refs[d][f, diagonal_at + unit] = value.astype(NARROW)

    close, far = shaped(n, freqs, 2, 2, half, tile), shaped(freqs, units, half, tile)
    return pl.pallas_call(
        kernel,
        in_specs=[IN_SMEM, UNREAD] + [IN_VMEM] * 2,
        out_specs=[IN_VMEM] * n,
        out_shape=[close] * 2 + [far] * (n - 2),
        compiler_params=params(),
        cost_estimate=cost(0, 4 * moved.size),
    )(place, after, moved, pairs)


def scatter_rows(place, groups, pairs, n, after):
    half, tile = pairs.shape[-2:]
    counts = [rows[0].shape[1] for rows in groups]
    freqs = sum(counts)
    pair_at, diagonal_at, units = far_units(n)

    def kernel(place_ref, after_ref, *refs):
        pairs_ref, out_ref = refs[-2:]
        me = place_ref[0]
        mine = me % 2

        def put(block, d, f, c, value):
            value = value.astype(NARROW)
            at = (me ^ block) * 2
            out_ref[at, me ^ d, f, c] = value[:half]
            out_ref[at + 1, me ^ d, f, c] = value[half:]

        def put_all(row_refs, d, f, own):
            ref = row_refs[d]
            if d < 2:
                for block in range(n):
                    for c in range(2):
                        put(block, d, f, c, square(ref, block, own, c))
                return
            for block in range(2, n):
                for c in range(2):
                    at = (block - 2) * 4 + 2 * c
                    put(block, d, f, c, square(ref, own, pl.ds(at, 2)))
            put(1, d, f, mine, square(ref, own, pl.ds(pair_at, 2)))
            put(1, d, f, 1 - mine, square(pairs_ref, (d ^ 1) - 2, f).T)
            last = ref[own, diagonal_at + 2].astype(WIDE)
            for c in range(2):
                put(0, d, f, c, unpack_diagonal(ref[own, diagonal_at + c].astype(WIDE), last, c))

        f = 0
        for group, count in enumerate(counts):
            for own in range(count):
                for d in range(n):
                    put_all(refs[group * n:(group + 1) * n], d, f, own)
                f += 1

    arrays = [array for rows in groups for array in rows]
    return pl.pallas_call(
        kernel,
        in_specs=[IN_SMEM, UNREAD] + [IN_VMEM] * (len(arrays) + 1),
        out_specs=IN_VMEM,
        out_shape=shaped(2 * n, n, freqs, 2, half, tile),
        compiler_params=params(),
        cost_estimate=cost(0, 0),
    )(place, after, *arrays, pairs)


def side_by_side(parts, after):
    shape = parts[0].shape
    n = len(parts)

    def kernel(after_ref, *refs):
        for part, ref in enumerate(refs[:n]):
            refs[n][:, part] = ref[...]

    return pl.pallas_call(
        kernel,
        in_specs=[UNREAD] + [IN_VMEM] * n,
        out_specs=IN_VMEM,
        out_shape=shaped(shape[0], n, *shape[1:]),
        compiler_params=params(),
        cost_estimate=cost(0, 4 * n * parts[0].size),
    )(after, *parts)


def apart(moved, start):
    shape = moved.shape
    n, freqs = shape[1], shape[2] - start

    def kernel(moved_ref, *out_refs):
        for part, ref in enumerate(out_refs):
            ref[...] = moved_ref[:, part, start:]

    return pl.pallas_call(
        kernel,
        in_specs=[IN_VMEM],
        out_specs=[IN_VMEM] * n,
        out_shape=[shaped(shape[0], freqs, *shape[3:])] * n,
        compiler_params=params(),
        cost_estimate=cost(0, 0),
    )(moved)


def gate(value, *after):
    return lax.optimization_barrier((value, *after))[0]


def chunk_sizes(per_group):
    return [per_group // 2, per_group - per_group // 2]


def swapped(value, gap):
    size = lax.axis_size("src")
    return lax.ppermute(value, "src", [(i, i ^ gap) for i in range(size)])


def spread(value):
    return lax.all_to_all(value, "rcv", split_axis=0, concat_axis=0, tiled=True)


def local_tiles(records, surface_operator):
    src_tiles, rcv_tiles, samples = records.shape
    freqs = surface_operator.shape[0]
    n = lax.axis_size("src")
    devices = 2 * n * n
    half = src_tiles // 2
    me, column = lax.axis_index("src"), lax.axis_index("rcv")
    place = me.astype(jnp.int32)[None]
    sizes = chunk_sizes(freqs // devices)
    starts = [devices * sum(sizes[:q]) for q in range(len(sizes))]

    forward, inverse = host_tables(freqs, samples)

    def rows_of(table, q):
        return table[starts[q]:starts[q] + devices * sizes[q]]

    def by_owner(table, q):
        rows = rows_of(table, q).reshape(2 * n, n, sizes[q] * 2, samples)
        return rows.swapaxes(0, 1).reshape(n, -1, samples)

    coeffs = []
    for q, size in enumerate(sizes):
        at = starts[q] + (column * n + me) * size
        coeffs.append(lax.dynamic_slice_in_dim(surface_operator, at, size, 0))

    def first_part(q):
        if q == 0:
            return jnp.asarray(by_owner(forward, 0))
        return jnp.asarray(rows_of(forward, q).reshape(1, -1, samples))

    def over_src(rows):
        return [rows[0]] + [swapped(rows[d], d) for d in range(1, n)]

    def pair_of(moved, q):
        theirs = 1 - me % 2
        pairs = []
        for d in range(2, n):
            at = ((me ^ 1) * 2, me ^ d, 0, theirs, 0, 0)
            pair = lax.dynamic_slice(moved, at, (2, 1, sizes[q], 1, half, src_tiles))
            pairs.append(pair.reshape(2, sizes[q], half, src_tiles))
        return swapped(jnp.stack(pairs), 1)

    def spread_chunk(spectrum, q):
        return spread(spectrum.reshape(2 * n, n, sizes[q], 2, half, src_tiles))

    def gather(moved, q, after):
        return gather_rows(place, moved, pair_of(moved, q), n, after)

    def pairs_of(groups):
        pair_at = far_units(n)[0]
        return jnp.stack(
            [
                jnp.concatenate([rows[d][:, pair_at:pair_at + 2] for rows in groups])
                for d in range(2, n)
            ]
        )

    def flat(moved):
        return moved.reshape(-1, half, src_tiles)

    *early, spectrum = forward_dft(place, records, [first_part(0), first_part(1)], place)
    early = over_src(early)
    moved1 = spread_chunk(spectrum, 1)
    sent1 = gather(moved1, 1, place)
    rows1 = over_src(sent1)
    parts = [part.reshape(2 * n, sizes[0], 2, half, src_tiles) for part in early]
    moved0 = spread(side_by_side(parts, sent1[0]))
    rest0 = predict(place, coeffs[0], [moved0], n, True, False, 1, sizes[0], sent1[0])
    sent0 = rest0[0]
    first0 = predict(place, coeffs[0], [moved0], n, True, False, 0, 1, sent0)
    sent0 = first0[0]
    first0 = over_src(first0)
    rest0 = over_src(rest0)
    back1 = predict(place, coeffs[1], rows1, n, False, True, 0, sizes[1], sent0)[0]
    moved = spread(gate(back1, *first0[1:]))
    first1 = over_src([moved[:, d, :1] for d in range(n)])
    rest1 = apart(moved, 1)
    sent1 = rest1[0]
    rest1 = over_src(rest1)
    pairs = swapped(pairs_of([first0, rest0]), 1)
    home0 = scatter_rows(place, [first0, rest0], pairs, n, sent1)
    home0 = spread(gate(home0, *first1[1:]))
    pieces = [[flat(home0)], [flat(x) for x in first1], [flat(x) for x in rest1]]
    last = by_owner(inverse, 1).reshape(n, 2 * n, sizes[1], 2, samples)
    tables = [
        jnp.asarray(rows_of(inverse, 0).reshape(1, -1, samples)),
        jnp.asarray(last[:, :, :1].reshape(n, -1, samples)),
        jnp.asarray(last[:, :, 1:].reshape(n, -1, samples)),
    ]
    return inverse_dft(place, pieces, tables)


def solution(mesh):
    placed = (P("src", "rcv", None), P())
    n_src, n_rcv = mesh.shape["src"], mesh.shape["rcv"]

    def local(records, surface_operator):
        src_tiles, rcv_tiles, _ = records.shape
        per_group = surface_operator.shape[0] // (n_src * n_rcv)
        square_tiles = n_rcv == 2 * n_src and src_tiles == 2 * rcv_tiles
        whole_lanes = src_tiles % 128 == 0 and n_src >= 4 and n_src & (n_src - 1) == 0
        if square_tiles and whole_lanes and per_group >= 4:
            return local_tiles(records, surface_operator)
        return local_general(records, surface_operator)

    return jax.shard_map(
        local, mesh=mesh, in_specs=placed, out_specs=P("src", "rcv", None), check_vma=False
    )
```

```python
import math

import jax
import jax.numpy as jnp
from jax import lax
from jax.sharding import PartitionSpec as P
from jax.experimental import pallas as pl
from jax.experimental.pallas import tpu as pltpu
import ml_dtypes
import numpy as np


def dft_tables(freqs, samples):
    freq_index = lax.broadcasted_iota(jnp.int32, (freqs, samples), 0)
    time_index = lax.broadcasted_iota(jnp.int32, (freqs, samples), 1)
    phase = (freq_index * time_index % samples).astype(jnp.float32)
    angle = phase * (2.0 * math.pi / samples)
    norming = 1.0 / math.sqrt(samples)
    cosine = jnp.cos(angle) * norming
    sine = jnp.sin(angle) * norming
    weights = jnp.where(freq_index == 0, 1.0, 2.0).astype(jnp.float32)
    forward = jnp.stack([cosine, -sine], axis=1).reshape(2 * freqs, samples)
    inverse = jnp.stack([weights * cosine, -weights * sine], axis=1).reshape(2 * freqs, samples)
    return (forward.astype(jnp.bfloat16), inverse.astype(jnp.bfloat16))


def batch_product(left, right):

    def mult(first_op, second_op):
        return jnp.einsum("nij,njk->nik", first_op, second_op, preferred_element_type=jnp.float32)

    real_part = mult(left[:, 0], right[:, 0]) - mult(left[:, 1], right[:, 1])
    imag_part = mult(left[:, 0], right[:, 1]) + mult(left[:, 1], right[:, 0])
    return (real_part, imag_part)


def predict_block(blocks, coeff):
    order = blocks.shape[2]
    recip = (
        0.5 * (blocks.astype(jnp.float32) + jnp.swapaxes(blocks, 2, 3).astype(jnp.float32))
    ).astype(jnp.bfloat16)
    factor = coeff / math.sqrt(order)
    real_k = factor[:, 0][:, None, None]
    imag_k = factor[:, 1][:, None, None]

    def scaled(product):
        return jnp.stack(
            [real_k * product[0] - imag_k * product[1], real_k * product[1] + imag_k * product[0]],
            axis=1,
        )

    first = scaled(batch_product(recip, recip)).astype(jnp.bfloat16)
    second = scaled(batch_product(recip, first)).astype(jnp.bfloat16)
    third = scaled(batch_product(recip, second))
    return (first.astype(jnp.float32) + second.astype(jnp.float32) + third).astype(jnp.bfloat16)


def local_general(records, surface_operator):
    src_tiles, rcv_tiles, samples = records.shape
    freqs = surface_operator.shape[0]
    n_src = lax.axis_size("src")
    n_rcv = lax.axis_size("rcv")
    per_group = freqs // (n_src * n_rcv)
    columns = src_tiles * rcv_tiles
    whole_src = n_src * src_tiles
    whole_rcv = n_rcv * rcv_tiles
    forward, inverse = dft_tables(freqs, samples)
    flat_traces = records.reshape(columns, samples)
    spectrum = jnp.einsum(
        "kt,nt->kn", forward, flat_traces, preferred_element_type=jnp.float32
    ).astype(jnp.bfloat16)
    group_index = lax.axis_index("src") * n_rcv + lax.axis_index("rcv")
    coeff = lax.dynamic_slice_in_dim(surface_operator, group_index * per_group, per_group, 0)
    moved = lax.all_to_all(
        spectrum.reshape(freqs, 2, 1, columns),
        ("src", "rcv"),
        split_axis=0,
        concat_axis=2,
        tiled=True,
    )
    blocks = moved.reshape(per_group, 2, n_src, n_rcv, src_tiles, rcv_tiles)
    blocks = blocks.transpose(0, 1, 2, 4, 3, 5).reshape(per_group, 2, whole_src, whole_rcv)
    predicted = predict_block(blocks, coeff)
    outgoing = predicted.reshape(per_group, 2, n_src, src_tiles, n_rcv, rcv_tiles).transpose(
        0, 1, 2, 4, 3, 5
    )
    returned = lax.all_to_all(
        outgoing.reshape(1, per_group, 2, n_src * n_rcv, columns),
        ("src", "rcv"),
        split_axis=3,
        concat_axis=0,
        tiled=True,
    )
    returned = returned.reshape(2 * freqs, columns)
    result = jnp.einsum("kn,kt->nt", returned, inverse, preferred_element_type=jnp.float32)
    return result.astype(jnp.bfloat16).reshape(src_tiles, rcv_tiles, samples)


NT = (((1,), (1,)), ((), ()))
TN = (((0,), (0,)), ((), ()))
VMEM_LIMIT = 56 * 2**20
ROWS = 16
BATCH = 4
WIDE = jnp.float32
NARROW = jnp.bfloat16
IN_VMEM = pl.BlockSpec(memory_space=pltpu.VMEM)
IN_SMEM = pl.BlockSpec(memory_space=pltpu.SMEM)
UNREAD = pl.BlockSpec(memory_space=pl.ANY)


def host_tables(freqs, samples):
    f = np.arange(freqs)[:, None]
    t = np.arange(samples)[None, :]
    angle = (f * t % samples) * (2.0 * math.pi / samples)
    norming = 1.0 / math.sqrt(samples)
    cosine = np.cos(angle) * norming
    sine = np.sin(angle) * norming
    weights = np.where(f == 0, 1.0, 2.0)
    forward = np.stack([cosine, -sine], axis=1)
    inverse = np.stack([weights * cosine, -weights * sine], axis=1)
    return [x.astype(np.float32).astype(ml_dtypes.bfloat16) for x in (forward, inverse)]


def params():
    return pltpu.CompilerParams(vmem_limit_bytes=VMEM_LIMIT)


def cost(flops, moved):
    return pl.CostEstimate(flops=0, bytes_accessed=0, transcendentals=0)


def shaped(*shape):
    return jax.ShapeDtypeStruct(shape, NARROW)


def forward_dft(place, records, tables, after):
    sources, receivers, samples = records.shape
    half = sources // 2
    width = 2 * receivers
    sizes = [table.shape[1] for table in tables for _ in range(table.shape[0])]
    rows = sum(sizes)

    def kernel(place_ref, after_ref, *refs):
        table_refs, records_ref = refs[:len(tables)], refs[len(tables)]
        out_refs, (turned, table) = refs[len(tables) + 1:-2], refs[-2:]

        @pl.when(pl.program_id(0) == 0)
        def _():
            at = 0
            for ref in table_refs:
                parts, size, _ = ref.shape
                for part in range(parts):
                    which = (place_ref[0] ^ part) if parts > 1 else 0
                    table[at:at + size, :] = ref[which]
                    at += size

        for p in range(0, ROWS, 2):
            traces = jnp.concatenate(
                [records_ref[s, p + d] for d in range(2) for s in range(2)], axis=0
            )
            found = lax.dot_general(table[...], traces, NT, preferred_element_type=WIDE)
            found = found.astype(NARROW)
            turned[p] = found[:, :width]
            turned[p + 1] = found[:, width:]
        at = 0
        for out_ref, size in zip(out_refs, sizes):
            out_ref[...] = jnp.swapaxes(turned[:, at:at + size, :], 0, 1)
            at += size

    return pl.pallas_call(
        kernel,
        grid=(half // ROWS,),
        in_specs=[IN_SMEM, UNREAD]
        + [pl.BlockSpec(table.shape, lambda i: (0, 0, 0)) for table in tables]
        + [pl.BlockSpec((2, ROWS, receivers, samples), lambda i: (0, i, 0, 0))],
        out_specs=[pl.BlockSpec((size, ROWS, width), lambda i: (0, i, 0)) for size in sizes],
        out_shape=[shaped(size, half, width) for size in sizes],
        scratch_shapes=[
            pltpu.VMEM((ROWS, rows, width), NARROW),
            pltpu.VMEM((rows, samples), NARROW),
        ],
        compiler_params=params(),
        cost_estimate=cost(2 * rows * records.size, 2 * (records.size + rows * half * width)),
    )(place, after, *tables, records.reshape(2, half, receivers, samples))


def inverse_dft(place, pieces, tables):
    half, width = pieces[0][0].shape[1:]
    receivers = width // 2
    samples = tables[0].shape[-1]
    spectra = [piece for group in pieces for piece in group]
    sizes = [piece.shape[0] for piece in spectra]
    rows = sum(sizes)

    def kernel(place_ref, *refs):
        table_refs = refs[:len(tables)]
        spectra_refs = refs[len(tables):len(tables) + len(spectra)]
        out_ref, turned, table = refs[len(tables) + len(spectra):]

        @pl.when(pl.program_id(0) == 0)
        def _():
            at = 0
            for table_ref, group in zip(table_refs, pieces):
                for part, piece in enumerate(group):
                    size = piece.shape[0]
                    which = (place_ref[0] ^ part) if len(group) > 1 else 0
                    table[at:at + size, :] = table_ref[which]
                    at += size

        at = 0
        for ref, size in zip(spectra_refs, sizes):
            turned[:, at:at + size, :] = jnp.swapaxes(ref[...], 0, 1)
            at += size
        for p in range(0, ROWS, BATCH):
            columns = [turned[p + q] for q in range(BATCH)]
            traces = lax.dot_general(
                jnp.concatenate(columns, axis=1), table[...], TN, preferred_element_type=WIDE
            ).astype(out_ref.dtype)
            for q in range(BATCH):
                out_ref[0, p + q] = traces[q * width:q * width + receivers]
                out_ref[1, p + q] = traces[q * width + receivers:(q + 1) * width]

    return pl.pallas_call(
        kernel,
        grid=(half // ROWS,),
        in_specs=[IN_SMEM]
        + [pl.BlockSpec(table.shape, lambda i: (0, 0, 0)) for table in tables]
        + [pl.BlockSpec((size, ROWS, width), lambda i: (0, i, 0)) for size in sizes],
        out_specs=pl.BlockSpec((2, ROWS, receivers, samples), lambda i: (0, i, 0, 0)),
        out_shape=shaped(2, half, receivers, samples),
        scratch_shapes=[
            pltpu.VMEM((ROWS, rows, width), NARROW),
            pltpu.VMEM((rows, samples), NARROW),
        ],
        compiler_params=params(),
        cost_estimate=cost(
            2 * rows * half * width * samples, 2 * half * width * (samples + rows)
        ),
    )(place, *tables, *spectra).reshape(2 * half, receivers, samples)


def swap_quarters(block):
    size = block.shape[0]
    half = size // 2
    rolled = pltpu.roll(block, half, 1)
    left = left_half(half, size)
    return jnp.concatenate(
        [
            jnp.where(left, block[:half], rolled[half:]),
            jnp.where(left, rolled[:half], block[half:]),
        ],
        axis=0,
    )


def left_half(rows, lanes):
    return lax.broadcasted_iota(jnp.int32, (rows, lanes), 1) < lanes // 2


def places(half):
    shape = (half, 2 * half)
    rows = lax.broadcasted_iota(jnp.int32, shape, 0)
    lanes = lax.broadcasted_iota(jnp.int32, shape, 1)
    left = lanes < half
    return rows, jnp.where(left, lanes, lanes - half), left


def pack_diagonals(real, imag):
    half = real.shape[0] // 2
    rows, lanes, left = places(half)
    packed, diagonals = [], []
    for block in (real, imag):
        lower = pltpu.roll(block[half:], half, 1)
        packed.append(jnp.where(left & (rows > lanes), lower, block[:half]))
        diagonals.append(jnp.where(rows == lanes, block[half:], 0.0))
    both = jnp.where(left, pltpu.roll(diagonals[0], half, 1), diagonals[1])
    both = jnp.sum(both, axis=0, keepdims=True)
    return packed[0], packed[1], jnp.broadcast_to(both, (ROWS, 2 * half))


def unpack_diagonal(packed, diagonals, c):
    half, size = packed.shape
    rows, lanes, left = places(half)
    mirrored = jnp.concatenate([packed, packed], axis=0).T
    diagonal = diagonals[:1]
    if c == 0:
        diagonal = pltpu.roll(jnp.broadcast_to(diagonal, (8, size)), half, 1)[:1]
    top = jnp.where(left & (rows > lanes), mirrored[:half], packed)
    last = jnp.where(rows > lanes, pltpu.roll(packed, half, 1), mirrored[:half])
    last = jnp.where(rows == lanes, diagonal, last)
    return jnp.concatenate([top, jnp.where(left, mirrored[half:], last)], axis=0)


def square(ref, *at):
    halves = ref[at] if at else ref[...]
    return halves.astype(WIDE).reshape(2 * halves.shape[-2], halves.shape[-1])


def dot(left, right):
    return jnp.dot(left, right, preferred_element_type=WIDE)


def series(real_k, imag_k, recip, first, out_block, tile):
    order = recip.shape[-1]
    panel = min(2 * tile, order)

    def scaled(real, imag):
        return real_k * real - imag_k * imag, real_k * imag + imag_k * real

    for start in range(0, order, panel):
        rows = pl.ds(start, panel)
        a, b = recip[0, rows, :], recip[1, rows, :]
        real, imag = scaled(
            dot(a, recip[0]) - dot(b, recip[1]), dot(a, recip[1]) + dot(b, recip[0])
        )
        first[0, rows, :] = real.astype(NARROW)
        first[1, rows, :] = imag.astype(NARROW)
    for start in range(0, order, panel):
        rows = pl.ds(start, panel)
        own = [first[c, rows, :].astype(WIDE) for c in range(2)]
        a, b = [(recip[c, rows, :].astype(WIDE) + own[c]).astype(NARROW) for c in range(2)]
        real, imag = scaled(
            dot(a, first[0]) - dot(b, first[1]), dot(a, first[1]) + dot(b, first[0])
        )
        real, imag = own[0] + real, own[1] + imag
        for row in range(0, panel, tile):
            for b in range(order // tile):
                at = (slice(row, row + tile), slice(b * tile, (b + 1) * tile))
                out_block(
                    (start + row) // tile, b, swap_quarters(real[at]), swap_quarters(imag[at])
                )


def far_rows(n, tile):
    pair = 2 * (n - 2) * tile
    return pair, pair + tile, pair + 2 * tile, pair + 2 * tile + ROWS


def other_rows(block, c, tile):
    at = (2 * (block - 2) + c) * tile
    return slice(at, at + tile)


def predict(place, coeff, moved, n, direct_in, direct_out, start, stop, after):
    freqs = stop - start
    half, tile = moved[0].shape[-2:]
    order = n * tile
    pair_at, diagonal_at, last_at, length = far_rows(n, tile)

    def kernel(place_ref, coeff_ref, after_ref, *refs):
        count = 1 if direct_in else n
        moved_refs, refs = refs[:count], refs[count:]
        count = 1 if direct_out else n
        out_refs, (recip, first) = refs[:count], refs[count:]
        me = place_ref[0]
        odd = me % 2 == 1

        def stacked(c, i, j):
            if direct_in:
                return square(moved_refs[0], pl.ds((j ^ me) * 2, 2), i, 0, c)
            if i < 2:
                return square(moved_refs[i], i ^ j, 0, c)
            return moved_refs[i][0, other_rows(i ^ j, c, tile)].astype(WIDE)

        def mean(c, a, b):
            if direct_in or a < 2 or (a ^ b) >= 2:
                return 0.5 * (stacked(c, a, b) + stacked(c, b, a).T)
            if a == b:
                ref = moved_refs[a]
                packed = ref[0, diagonal_at + c * half:diagonal_at + (c + 1) * half]
                diagonals = ref[0, last_at:length]
                return unpack_diagonal(packed.astype(WIDE), diagonals.astype(WIDE), c)
            here = moved_refs[a][0, pair_at:pair_at + tile].astype(WIDE)
            there = moved_refs[b][0, pair_at:pair_at + tile].astype(WIDE).T
            return jnp.where(odd == (c == 0), here, there)

        for c in range(2):
            for a in range(n):
                for b in range(a + 1):
                    block = swap_quarters(mean(c, a, b))
                    rows, columns = slice(a * tile, (a + 1) * tile), slice(b * tile, (b + 1) * tile)
                    recip[c, rows, columns] = block.astype(NARROW)
                    if a != b:
                        recip[c, columns, rows] = block.T.astype(NARROW)

        def out_block(a, b, real, imag):
            gap = a ^ b
            if not direct_out and a >= 2 and gap == 1:
                own = jnp.where(odd == (a % 2 == 0), imag, real).astype(NARROW)
                out_refs[a][0, pair_at:pair_at + tile] = own
                return
            if not direct_out and a >= 2 and gap == 0:
                at = diagonal_at
                for value in pack_diagonals(real, imag):
                    out_refs[a][0, at:at + value.shape[0]] = value.astype(NARROW)
                    at += value.shape[0]
                return
            for c, value in enumerate((real, imag)):
                value = value.astype(NARROW)
                if not direct_out and a >= 2:
                    out_refs[a][0, other_rows(gap, c, tile)] = value
                    continue
                for h in range(2):
                    part = value[h * half:(h + 1) * half]
                    if direct_out:
                        out_refs[0][(b ^ me) * 2 + h, a, 0, c] = part
                    else:
                        out_refs[a][gap, 0, c, h] = part

        index = pl.program_id(0) + start
        series(coeff_ref[index, 0], coeff_ref[index, 1], recip, first, out_block, tile)

    whole = (2 * n, n, freqs, 2, half, tile)
    close = (n, freqs, 2, 2, half, tile)
    far = (freqs, length, tile)
    split_shapes = [shaped(*close)] * 2 + [shaped(*far)] * (n - 2)

    def specs(direct, first):
        if direct:
            block = (2 * n, n, 1, 2, half, tile)
            return [pl.BlockSpec(block, lambda i: (0, 0, i + first, 0, 0, 0))]
        close = pl.BlockSpec((n, 1, 2, 2, half, tile), lambda i: (0, i + first, 0, 0, 0, 0))
        far = pl.BlockSpec((1, length, tile), lambda i: (i + first, 0, 0))
        return [close] * 2 + [far] * (n - 2)

    return pl.pallas_call(
        kernel,
        grid=(freqs,),
        in_specs=[IN_SMEM, IN_SMEM, UNREAD] + specs(direct_in, start),
        out_specs=specs(direct_out, 0),
        out_shape=[shaped(*whole)] if direct_out else split_shapes,
        scratch_shapes=[pltpu.VMEM((2, order, order), NARROW)] * 2,
        compiler_params=params(),
        cost_estimate=cost(16 * freqs * order**3, 16 * freqs * order**2),
    )(place, coeff / math.sqrt(order), after, *moved)


def gather_rows(place, moved, pairs, n, after):
    _, _, freqs, _, half, tile = moved.shape
    pair_at, diagonal_at, last_at, length = far_rows(n, tile)

    def kernel(place_ref, after_ref, moved_ref, pairs_ref, *out_refs):
        me = place_ref[0]
        mine = me % 2

        def halves(block):
            return pl.ds((me ^ block) * 2, 2)

        for d in range(2):
            for block in range(n):
                for f in range(freqs):
                    for c in range(2):
                        out_refs[d][block, f, c] = moved_ref[halves(block), me ^ d, f, c]
        for d in range(2, n):
            for f in range(freqs):
                for block in range(2, n):
                    for c in range(2):
                        rows = moved_ref[halves(block), me ^ d, f, c].reshape(tile, tile)
                        out_refs[d][f, other_rows(block, c, tile)] = rows
                here = square(moved_ref, halves(1), me ^ d, f, mine)
                there = square(pairs_ref, (d ^ 1) - 2, slice(None), f)
                mean = (0.5 * (here + there.T)).astype(NARROW)
                out_refs[d][f, pair_at:pair_at + tile] = mean
                means = []
                for c in range(2):
                    block = square(moved_ref, halves(0), me ^ d, f, c)
                    means.append(0.5 * (block + block.T))
                at = diagonal_at
                for value in pack_diagonals(*means):
                    out_refs[d][f, at:at + value.shape[0]] = value.astype(NARROW)
                    at += value.shape[0]

    close, far = shaped(n, freqs, 2, 2, half, tile), shaped(freqs, length, tile)
    return pl.pallas_call(
        kernel,
        in_specs=[IN_SMEM, UNREAD] + [IN_VMEM] * 2,
        out_specs=[IN_VMEM] * n,
        out_shape=[close] * 2 + [far] * (n - 2),
        compiler_params=params(),
        cost_estimate=cost(0, 4 * moved.size),
    )(place, after, moved, pairs)


def scatter_rows(place, groups, pairs, n, after):
    tile = pairs.shape[-1]
    half = tile // 2
    counts = [rows[0].shape[1] for rows in groups]
    freqs = sum(counts)
    pair_at, diagonal_at, last_at, length = far_rows(n, tile)

    def kernel(place_ref, after_ref, *refs):
        pairs_ref, out_ref = refs[-2:]
        me = place_ref[0]
        mine = me % 2

        def put(block, d, f, c, value):
            value = value.astype(NARROW)
            at = (me ^ block) * 2
            out_ref[at, me ^ d, f, c] = value[:half]
            out_ref[at + 1, me ^ d, f, c] = value[half:]

        def put_all(row_refs, d, f, own):
            ref = row_refs[d]
            if d < 2:
                for block in range(n):
                    for c in range(2):
                        put(block, d, f, c, square(ref, block, own, c))
                return
            for block in range(2, n):
                for c in range(2):
                    put(block, d, f, c, ref[own, other_rows(block, c, tile)])
            put(1, d, f, mine, ref[own, pair_at:pair_at + tile])
            put(1, d, f, 1 - mine, pairs_ref[(d ^ 1) - 2, f].astype(WIDE).T)
            last = ref[own, last_at:length].astype(WIDE)
            for c in range(2):
                packed = ref[own, diagonal_at + c * half:diagonal_at + (c + 1) * half]
                put(0, d, f, c, unpack_diagonal(packed.astype(WIDE), last, c))

        f = 0
        for group, count in enumerate(counts):
            for own in range(count):
                for d in range(n):
                    put_all(refs[group * n:(group + 1) * n], d, f, own)
                f += 1

    arrays = [array for rows in groups for array in rows]
    return pl.pallas_call(
        kernel,
        in_specs=[IN_SMEM, UNREAD] + [IN_VMEM] * (len(arrays) + 1),
        out_specs=IN_VMEM,
        out_shape=shaped(2 * n, n, freqs, 2, half, tile),
        compiler_params=params(),
        cost_estimate=cost(0, 0),
    )(place, after, *arrays, pairs)


def side_by_side(parts, after):
    shape = parts[0].shape
    n = len(parts)

    def kernel(after_ref, *refs):
        for part, ref in enumerate(refs[:n]):
            refs[n][:, part] = ref[...]

    return pl.pallas_call(
        kernel,
        in_specs=[UNREAD] + [IN_VMEM] * n,
        out_specs=IN_VMEM,
        out_shape=shaped(shape[0], n, *shape[1:]),
        compiler_params=params(),
        cost_estimate=cost(0, 4 * n * parts[0].size),
    )(after, *parts)


def apart(moved, start):
    shape = moved.shape
    n, freqs = shape[1], shape[2] - start

    def kernel(moved_ref, *out_refs):
        for part, ref in enumerate(out_refs):
            ref[...] = moved_ref[:, part, start:]

    return pl.pallas_call(
        kernel,
        in_specs=[IN_VMEM],
        out_specs=[IN_VMEM] * n,
        out_shape=[shaped(shape[0], freqs, *shape[3:])] * n,
        compiler_params=params(),
        cost_estimate=cost(0, 0),
    )(moved)


def gate(value, *after):
    return lax.optimization_barrier((value, *after))[0]


def chunk_sizes(per_group):
    return [per_group // 2, per_group - per_group // 2]


def swapped(value, gap):
    size = lax.axis_size("src")
    return lax.ppermute(value, "src", [(i, i ^ gap) for i in range(size)])


def spread(value):
    return lax.all_to_all(value, "rcv", split_axis=0, concat_axis=0, tiled=True)


def local_tiles(records, surface_operator):
    src_tiles, rcv_tiles, samples = records.shape
    freqs = surface_operator.shape[0]
    n = lax.axis_size("src")
    devices = 2 * n * n
    half = src_tiles // 2
    me, column = lax.axis_index("src"), lax.axis_index("rcv")
    place = me.astype(jnp.int32)[None]
    sizes = chunk_sizes(freqs // devices)
    starts = [devices * sum(sizes[:q]) for q in range(len(sizes))]

    forward, inverse = host_tables(freqs, samples)

    def rows_of(table, q):
        return table[starts[q]:starts[q] + devices * sizes[q]]

    def by_owner(table, q):
        rows = rows_of(table, q).reshape(2 * n, n, sizes[q] * 2, samples)
        return rows.swapaxes(0, 1).reshape(n, -1, samples)

    coeffs = []
    for q, size in enumerate(sizes):
        at = starts[q] + (column * n + me) * size
        coeffs.append(lax.dynamic_slice_in_dim(surface_operator, at, size, 0))

    def first_part(q):
        if q == 0:
            return jnp.asarray(by_owner(forward, 0))
        return jnp.asarray(rows_of(forward, q).reshape(1, -1, samples))

    def over_src(rows):
        return [rows[0]] + [swapped(rows[d], d) for d in range(1, n)]

    def pair_of(moved, q):
        theirs = 1 - me % 2
        pairs = []
        for d in range(2, n):
            at = ((me ^ 1) * 2, me ^ d, 0, theirs, 0, 0)
            pair = lax.dynamic_slice(moved, at, (2, 1, sizes[q], 1, half, src_tiles))
            pairs.append(pair.reshape(2, sizes[q], half, src_tiles))
        return swapped(jnp.stack(pairs), 1)

    def spread_chunk(spectrum, q):
        return spread(spectrum.reshape(2 * n, n, sizes[q], 2, half, src_tiles))

    def gather(moved, q, after):
        return gather_rows(place, moved, pair_of(moved, q), n, after)

    def pairs_of(groups):
        pair_at = far_rows(n, src_tiles)[0]
        return jnp.stack(
            [
                jnp.concatenate([rows[d][:, pair_at:pair_at + src_tiles] for rows in groups])
                for d in range(2, n)
            ]
        )

    def flat(moved):
        return moved.reshape(-1, half, src_tiles)

    *early, spectrum = forward_dft(place, records, [first_part(0), first_part(1)], place)
    early = over_src(early)
    moved1 = spread_chunk(spectrum, 1)
    sent1 = gather(moved1, 1, place)
    rows1 = over_src(sent1)
    parts = [part.reshape(2 * n, sizes[0], 2, half, src_tiles) for part in early]
    moved0 = spread(side_by_side(parts, sent1[0]))
    rest0 = predict(place, coeffs[0], [moved0], n, True, False, 1, sizes[0], sent1[0])
    sent0 = rest0[0]
    first0 = predict(place, coeffs[0], [moved0], n, True, False, 0, 1, sent0)
    sent0 = first0[0]
    first0 = over_src(first0)
    rest0 = over_src(rest0)
    back1 = predict(place, coeffs[1], rows1, n, False, True, 0, sizes[1], sent0)[0]
    moved = spread(gate(back1, *first0[1:]))
    first1 = over_src([moved[:, d, :1] for d in range(n)])
    rest1 = apart(moved, 1)
    sent1 = rest1[0]
    rest1 = over_src(rest1)
    pairs = swapped(pairs_of([first0, rest0]), 1)
    home0 = scatter_rows(place, [first0, rest0], pairs, n, sent1)
    home0 = spread(gate(home0, *first1[1:]))
    pieces = [[flat(home0)], [flat(x) for x in first1], [flat(x) for x in rest1]]
    last = by_owner(inverse, 1).reshape(n, 2 * n, sizes[1], 2, samples)
    tables = [
        jnp.asarray(rows_of(inverse, 0).reshape(1, -1, samples)),
        jnp.asarray(last[:, :, :1].reshape(n, -1, samples)),
        jnp.asarray(last[:, :, 1:].reshape(n, -1, samples)),
    ]
    return inverse_dft(place, pieces, tables)


def solution(mesh):
    placed = (P("src", "rcv", None), P())
    n_src, n_rcv = mesh.shape["src"], mesh.shape["rcv"]

    def local(records, surface_operator):
        src_tiles, rcv_tiles, _ = records.shape
        per_group = surface_operator.shape[0] // (n_src * n_rcv)
        square_tiles = n_rcv == 2 * n_src and src_tiles == 2 * rcv_tiles
        whole_lanes = src_tiles % 128 == 0 and n_src >= 4 and n_src & (n_src - 1) == 0
        if square_tiles and whole_lanes and per_group >= 4:
            return local_tiles(records, surface_operator)
        return local_general(records, surface_operator)

    return jax.shard_map(
        local, mesh=mesh, in_specs=placed, out_specs=P("src", "rcv", None), check_vma=False
    )
```

```python
import math

import jax
import jax.numpy as jnp
from jax import lax
from jax.sharding import PartitionSpec as P
from jax.experimental import pallas as pl
from jax.experimental.pallas import tpu as pltpu
import ml_dtypes
import numpy as np


def dft_tables(freqs, samples):
    freq_index = lax.broadcasted_iota(jnp.int32, (freqs, samples), 0)
    time_index = lax.broadcasted_iota(jnp.int32, (freqs, samples), 1)
    phase = (freq_index * time_index % samples).astype(jnp.float32)
    angle = phase * (2.0 * math.pi / samples)
    norming = 1.0 / math.sqrt(samples)
    cosine = jnp.cos(angle) * norming
    sine = jnp.sin(angle) * norming
    weights = jnp.where(freq_index == 0, 1.0, 2.0).astype(jnp.float32)
    forward = jnp.stack([cosine, -sine], axis=1).reshape(2 * freqs, samples)
    inverse = jnp.stack([weights * cosine, -weights * sine], axis=1).reshape(2 * freqs, samples)
    return (forward.astype(jnp.bfloat16), inverse.astype(jnp.bfloat16))


def batch_product(left, right):

    def mult(first_op, second_op):
        return jnp.einsum("nij,njk->nik", first_op, second_op, preferred_element_type=jnp.float32)

    real_part = mult(left[:, 0], right[:, 0]) - mult(left[:, 1], right[:, 1])
    imag_part = mult(left[:, 0], right[:, 1]) + mult(left[:, 1], right[:, 0])
    return (real_part, imag_part)


def predict_block(blocks, coeff):
    order = blocks.shape[2]
    recip = (
        0.5 * (blocks.astype(jnp.float32) + jnp.swapaxes(blocks, 2, 3).astype(jnp.float32))
    ).astype(jnp.bfloat16)
    factor = coeff / math.sqrt(order)
    real_k = factor[:, 0][:, None, None]
    imag_k = factor[:, 1][:, None, None]

    def scaled(product):
        return jnp.stack(
            [real_k * product[0] - imag_k * product[1], real_k * product[1] + imag_k * product[0]],
            axis=1,
        )

    first = scaled(batch_product(recip, recip)).astype(jnp.bfloat16)
    second = scaled(batch_product(recip, first)).astype(jnp.bfloat16)
    third = scaled(batch_product(recip, second))
    return (first.astype(jnp.float32) + second.astype(jnp.float32) + third).astype(jnp.bfloat16)


def local_general(records, surface_operator):
    src_tiles, rcv_tiles, samples = records.shape
    freqs = surface_operator.shape[0]
    n_src = lax.axis_size("src")
    n_rcv = lax.axis_size("rcv")
    per_group = freqs // (n_src * n_rcv)
    columns = src_tiles * rcv_tiles
    whole_src = n_src * src_tiles
    whole_rcv = n_rcv * rcv_tiles
    forward, inverse = dft_tables(freqs, samples)
    flat_traces = records.reshape(columns, samples)
    spectrum = jnp.einsum(
        "kt,nt->kn", forward, flat_traces, preferred_element_type=jnp.float32
    ).astype(jnp.bfloat16)
    group_index = lax.axis_index("src") * n_rcv + lax.axis_index("rcv")
    coeff = lax.dynamic_slice_in_dim(surface_operator, group_index * per_group, per_group, 0)
    moved = lax.all_to_all(
        spectrum.reshape(freqs, 2, 1, columns),
        ("src", "rcv"),
        split_axis=0,
        concat_axis=2,
        tiled=True,
    )
    blocks = moved.reshape(per_group, 2, n_src, n_rcv, src_tiles, rcv_tiles)
    blocks = blocks.transpose(0, 1, 2, 4, 3, 5).reshape(per_group, 2, whole_src, whole_rcv)
    predicted = predict_block(blocks, coeff)
    outgoing = predicted.reshape(per_group, 2, n_src, src_tiles, n_rcv, rcv_tiles).transpose(
        0, 1, 2, 4, 3, 5
    )
    returned = lax.all_to_all(
        outgoing.reshape(1, per_group, 2, n_src * n_rcv, columns),
        ("src", "rcv"),
        split_axis=3,
        concat_axis=0,
        tiled=True,
    )
    returned = returned.reshape(2 * freqs, columns)
    result = jnp.einsum("kn,kt->nt", returned, inverse, preferred_element_type=jnp.float32)
    return result.astype(jnp.bfloat16).reshape(src_tiles, rcv_tiles, samples)


NT = (((1,), (1,)), ((), ()))
TN = (((0,), (0,)), ((), ()))
VMEM_LIMIT = 56 * 2**20
ROWS = 16
BATCH = 4
WIDE = jnp.float32
NARROW = jnp.bfloat16
IN_VMEM = pl.BlockSpec(memory_space=pltpu.VMEM)
IN_SMEM = pl.BlockSpec(memory_space=pltpu.SMEM)
UNREAD = pl.BlockSpec(memory_space=pl.ANY)


def host_tables(freqs, samples):
    f = np.arange(freqs)[:, None]
    t = np.arange(samples)[None, :]
    angle = (f * t % samples) * (2.0 * math.pi / samples)
    norming = 1.0 / math.sqrt(samples)
    cosine = np.cos(angle) * norming
    sine = np.sin(angle) * norming
    weights = np.where(f == 0, 1.0, 2.0)
    forward = np.stack([cosine, -sine], axis=1)
    inverse = np.stack([weights * cosine, -weights * sine], axis=1)
    return [x.astype(np.float32).astype(ml_dtypes.bfloat16) for x in (forward, inverse)]


def params():
    return pltpu.CompilerParams(vmem_limit_bytes=VMEM_LIMIT)


def cost(flops, moved):
    return pl.CostEstimate(flops=0, bytes_accessed=0, transcendentals=0)


def shaped(*shape):
    return jax.ShapeDtypeStruct(shape, NARROW)


def forward_dft(place, records, tables, after):
    sources, receivers, samples = records.shape
    half = sources // 2
    width = 2 * receivers
    sizes = [table.shape[1] for table in tables for _ in range(table.shape[0])]
    rows = sum(sizes)

    def kernel(place_ref, after_ref, *refs):
        table_refs, records_ref = refs[:len(tables)], refs[len(tables)]
        out_refs, (turned, table) = refs[len(tables) + 1:-2], refs[-2:]

        @pl.when(pl.program_id(0) == 0)
        def _():
            at = 0
            for ref in table_refs:
                parts, size, _ = ref.shape
                for part in range(parts):
                    which = (place_ref[0] ^ part) if parts > 1 else 0
                    table[at:at + size, :] = ref[which]
                    at += size

        for p in range(0, ROWS, 2):
            traces = jnp.concatenate(
                [records_ref[s, p + d] for d in range(2) for s in range(2)], axis=0
            )
            found = lax.dot_general(table[...], traces, NT, preferred_element_type=WIDE)
            found = found.astype(NARROW)
            turned[p] = found[:, :width]
            turned[p + 1] = found[:, width:]
        at = 0
        for out_ref, size in zip(out_refs, sizes):
            out_ref[...] = jnp.swapaxes(turned[:, at:at + size, :], 0, 1)
            at += size

    return pl.pallas_call(
        kernel,
        grid=(half // ROWS,),
        in_specs=[IN_SMEM, UNREAD]
        + [pl.BlockSpec(table.shape, lambda i: (0, 0, 0)) for table in tables]
        + [pl.BlockSpec((2, ROWS, receivers, samples), lambda i: (0, i, 0, 0))],
        out_specs=[pl.BlockSpec((size, ROWS, width), lambda i: (0, i, 0)) for size in sizes],
        out_shape=[shaped(size, half, width) for size in sizes],
        scratch_shapes=[
            pltpu.VMEM((ROWS, rows, width), NARROW),
            pltpu.VMEM((rows, samples), NARROW),
        ],
        compiler_params=params(),
        cost_estimate=cost(2 * rows * records.size, 2 * (records.size + rows * half * width)),
    )(place, after, *tables, records.reshape(2, half, receivers, samples))


def inverse_dft(place, pieces, tables):
    half, width = pieces[0][0].shape[1:]
    receivers = width // 2
    samples = tables[0].shape[-1]
    spectra = [piece for group in pieces for piece in group]
    sizes = [piece.shape[0] for piece in spectra]
    rows = sum(sizes)

    def kernel(place_ref, *refs):
        table_refs = refs[:len(tables)]
        spectra_refs = refs[len(tables):len(tables) + len(spectra)]
        out_ref, turned, table = refs[len(tables) + len(spectra):]

        @pl.when(pl.program_id(0) == 0)
        def _():
            at = 0
            for table_ref, group in zip(table_refs, pieces):
                for part, piece in enumerate(group):
                    size = piece.shape[0]
                    which = (place_ref[0] ^ part) if len(group) > 1 else 0
                    table[at:at + size, :] = table_ref[which]
                    at += size

        at = 0
        for ref, size in zip(spectra_refs, sizes):
            turned[:, at:at + size, :] = jnp.swapaxes(ref[...], 0, 1)
            at += size
        for p in range(0, ROWS, BATCH):
            columns = [turned[p + q] for q in range(BATCH)]
            traces = lax.dot_general(
                jnp.concatenate(columns, axis=1), table[...], TN, preferred_element_type=WIDE
            ).astype(out_ref.dtype)
            for q in range(BATCH):
                out_ref[0, p + q] = traces[q * width:q * width + receivers]
                out_ref[1, p + q] = traces[q * width + receivers:(q + 1) * width]

    return pl.pallas_call(
        kernel,
        grid=(half // ROWS,),
        in_specs=[IN_SMEM]
        + [pl.BlockSpec(table.shape, lambda i: (0, 0, 0)) for table in tables]
        + [pl.BlockSpec((size, ROWS, width), lambda i: (0, i, 0)) for size in sizes],
        out_specs=pl.BlockSpec((2, ROWS, receivers, samples), lambda i: (0, i, 0, 0)),
        out_shape=shaped(2, half, receivers, samples),
        scratch_shapes=[
            pltpu.VMEM((ROWS, rows, width), NARROW),
            pltpu.VMEM((rows, samples), NARROW),
        ],
        compiler_params=params(),
        cost_estimate=cost(
            2 * rows * half * width * samples, 2 * half * width * (samples + rows)
        ),
    )(place, *tables, *spectra).reshape(2 * half, receivers, samples)


def swap_quarters(block):
    half = block.shape[0] // 2
    return jnp.concatenate(
        [
            jnp.concatenate([block[:half, :half], block[half:, :half]], axis=1),
            jnp.concatenate([block[:half, half:], block[half:, half:]], axis=1),
        ],
        axis=0,
    )


def left_half(rows, lanes):
    return lax.broadcasted_iota(jnp.int32, (rows, lanes), 1) < lanes // 2


def places(half):
    shape = (half, 2 * half)
    rows = lax.broadcasted_iota(jnp.int32, shape, 0)
    lanes = lax.broadcasted_iota(jnp.int32, shape, 1)
    left = lanes < half
    return rows, jnp.where(left, lanes, lanes - half), left


def pack_diagonals(real, imag):
    half = real.shape[0] // 2
    rows, lanes, left = places(half)
    packed, diagonals = [], []
    for block in (real, imag):
        lower = pltpu.roll(block[half:], half, 1)
        packed.append(jnp.where(left & (rows > lanes), lower, block[:half]))
        diagonals.append(jnp.where(rows == lanes, block[half:], 0.0))
    both = jnp.where(left, pltpu.roll(diagonals[0], half, 1), diagonals[1])
    both = jnp.sum(both, axis=0, keepdims=True)
    return packed[0], packed[1], jnp.broadcast_to(both, (ROWS, 2 * half))


def unpack_diagonal(packed, diagonals, c):
    half, size = packed.shape
    rows, lanes, left = places(half)
    mirrored = jnp.concatenate([packed, packed], axis=0).T
    diagonal = diagonals[:1]
    if c == 0:
        diagonal = pltpu.roll(jnp.broadcast_to(diagonal, (8, size)), half, 1)[:1]
    top = jnp.where(left & (rows > lanes), mirrored[:half], packed)
    last = jnp.where(rows > lanes, pltpu.roll(packed, half, 1), mirrored[:half])
    last = jnp.where(rows == lanes, diagonal, last)
    return jnp.concatenate([top, jnp.where(left, mirrored[half:], last)], axis=0)


def square(ref, *at):
    halves = ref[at] if at else ref[...]
    return halves.astype(WIDE).reshape(2 * halves.shape[-2], halves.shape[-1])


def dot(left, right):
    return jnp.dot(left, right, preferred_element_type=WIDE)


def series(real_k, imag_k, recip, first, out_block, tile):
    order = recip.shape[-1]
    panel = min(2 * tile, order)

    def scaled(real, imag):
        return real_k * real - imag_k * imag, real_k * imag + imag_k * real

    for start in range(0, order, panel):
        rows = pl.ds(start, panel)
        a, b = recip[0, rows, :], recip[1, rows, :]
        real, imag = scaled(
            dot(a, recip[0]) - dot(b, recip[1]), dot(a, recip[1]) + dot(b, recip[0])
        )
        first[0, rows, :] = real.astype(NARROW)
        first[1, rows, :] = imag.astype(NARROW)
    for start in range(0, order, panel):
        rows = pl.ds(start, panel)
        own = [first[c, rows, :].astype(WIDE) for c in range(2)]
        a, b = [(recip[c, rows, :].astype(WIDE) + own[c]).astype(NARROW) for c in range(2)]
        real, imag = scaled(
            dot(a, first[0]) - dot(b, first[1]), dot(a, first[1]) + dot(b, first[0])
        )
        real, imag = own[0] + real, own[1] + imag
        for row in range(0, panel, tile):
            for b in range(order // tile):
                at = (slice(row, row + tile), slice(b * tile, (b + 1) * tile))
                out_block(
                    (start + row) // tile, b, swap_quarters(real[at].astype(NARROW)), swap_quarters(imag[at].astype(NARROW))
                )


def far_rows(n, tile):
    pair = 2 * (n - 2) * tile
    return pair, pair + tile, pair + 2 * tile, pair + 2 * tile + ROWS


def other_rows(block, c, tile):
    at = (2 * (block - 2) + c) * tile
    return slice(at, at + tile)


def predict(place, coeff, moved, n, direct_in, direct_out, start, stop, after):
    freqs = stop - start
    half, tile = moved[0].shape[-2:]
    order = n * tile
    pair_at, diagonal_at, last_at, length = far_rows(n, tile)

    def kernel(place_ref, coeff_ref, after_ref, *refs):
        count = 1 if direct_in else n + 1
        moved_refs, refs = refs[:count], refs[count:]
        ahead = pl.program_id(0) == 0

        def far(i, rows):
            if i > 2:
                return moved_refs[i + 1][0, rows].astype(WIDE)
            one, other = (moved_refs[k][0, rows].astype(WIDE) for k in (2, 3))
            return jnp.where(ahead, one, other)

        count = 1 if direct_out else n
        out_refs, (recip, first) = refs[:count], refs[count:]
        me = place_ref[0]
        odd = me % 2 == 1

        def stacked(c, i, j):
            if direct_in:
                return square(moved_refs[0], pl.ds((j ^ me) * 2, 2), i, 0, c)
            if i < 2:
                return square(moved_refs[i], i ^ j, 0, c)
            return far(i, other_rows(i ^ j, c, tile))

        def mean(c, a, b):
            if direct_in or a < 2 or (a ^ b) >= 2:
                turned = stacked(c, b, a).astype(NARROW).T.astype(WIDE)
                return 0.5 * (stacked(c, a, b) + turned)
            if a == b:
                at = diagonal_at + c * half
                packed = far(a, slice(at, at + half))
                return unpack_diagonal(packed, far(a, slice(last_at, length)), c)
            here = far(a, slice(pair_at, pair_at + tile))
            there = far(b, slice(pair_at, pair_at + tile)).T
            return jnp.where(odd == (c == 0), here, there)

        for c in range(2):
            for a in range(n):
                for b in range(a + 1):
                    block = swap_quarters(mean(c, a, b).astype(NARROW))
                    rows, columns = slice(a * tile, (a + 1) * tile), slice(b * tile, (b + 1) * tile)
                    recip[c, rows, columns] = block.astype(NARROW)
                    if a != b:
                        recip[c, columns, rows] = block.astype(NARROW).T

        def out_block(a, b, real, imag):
            gap = a ^ b
            if not direct_out and a >= 2 and gap == 1:
                own = jnp.where(odd == (a % 2 == 0), imag, real).astype(NARROW)
                out_refs[a][0, pair_at:pair_at + tile] = own
                return
            if not direct_out and a >= 2 and gap == 0:
                at = diagonal_at
                for value in pack_diagonals(real.astype(WIDE), imag.astype(WIDE)):
                    out_refs[a][0, at:at + value.shape[0]] = value.astype(NARROW)
                    at += value.shape[0]
                return
            for c, value in enumerate((real, imag)):
                value = value.astype(NARROW)
                if not direct_out and a >= 2:
                    out_refs[a][0, other_rows(gap, c, tile)] = value
                    continue
                for h in range(2):
                    part = value[h * half:(h + 1) * half]
                    if direct_out:
                        out_refs[0][(b ^ me) * 2 + h, a, 0, c] = part
                    else:
                        out_refs[a][gap, 0, c, h] = part

        index = pl.program_id(0) + start
        series(coeff_ref[index, 0], coeff_ref[index, 1], recip, first, out_block, tile)

    whole = (2 * n, n, freqs, 2, half, tile)
    close = (n, freqs, 2, 2, half, tile)
    far = (freqs, length, tile)
    split_shapes = [shaped(*close)] * 2 + [shaped(*far)] * (n - 2)

    def specs(direct, first, split):
        if direct:
            block = (2 * n, n, 1, 2, half, tile)
            return [pl.BlockSpec(block, lambda i: (0, 0, i + first, 0, 0, 0))]
        close = pl.BlockSpec((n, 1, 2, 2, half, tile), lambda i: (0, i + first, 0, 0, 0, 0))
        far = pl.BlockSpec((1, length, tile), lambda i: (i + first, 0, 0))
        if not split:
            return [close] * 2 + [far] * (n - 2)
        one = pl.BlockSpec((1, length, tile), lambda i: (0, 0, 0))
        others = pl.BlockSpec((1, length, tile), lambda i: (jnp.maximum(i - 1, 0), 0, 0))
        return [close] * 2 + [one, others] + [far] * (n - 3)

    return pl.pallas_call(
        kernel,
        grid=(freqs,),
        in_specs=[IN_SMEM, IN_SMEM, UNREAD] + specs(direct_in, start, True),
        out_specs=specs(direct_out, 0, False),
        out_shape=[shaped(*whole)] if direct_out else split_shapes,
        scratch_shapes=[pltpu.VMEM((2, order, order), NARROW)] * 2,
        compiler_params=params(),
        cost_estimate=cost(16 * freqs * order**3, 16 * freqs * order**2),
    )(place, coeff / math.sqrt(order), after, *moved)


def gather_rows(place, moved, pairs, n, after):
    _, _, freqs, _, half, tile = moved.shape
    pair_at, diagonal_at, last_at, length = far_rows(n, tile)

    def kernel(place_ref, after_ref, moved_ref, pairs_ref, *out_refs):
        me = place_ref[0]
        mine = me % 2

        def halves(block):
            return pl.ds((me ^ block) * 2, 2)

        for d in range(2):
            for block in range(n):
                for f in range(freqs):
                    for c in range(2):
                        out_refs[d][block, f, c] = moved_ref[halves(block), me ^ d, f, c]
        for d in range(2, n):
            for f in range(freqs):
                out_ref, own = (out_refs[d + 1], f) if d > 2 or f else (out_refs[2], 0)
                own = f - 1 if d == 2 and f else own
                for block in range(2, n):
                    for c in range(2):
                        rows = moved_ref[halves(block), me ^ d, f, c].reshape(tile, tile)
                        out_ref[own, other_rows(block, c, tile)] = rows
                here = square(moved_ref, halves(1), me ^ d, f, mine)
                there = square(pairs_ref, (d ^ 1) - 2, slice(None), f)
                mean = (0.5 * (here + there.T)).astype(NARROW)
                out_ref[own, pair_at:pair_at + tile] = mean
                means = []
                for c in range(2):
                    block = square(moved_ref, halves(0), me ^ d, f, c)
                    means.append(0.5 * (block + block.T))
                at = diagonal_at
                for value in pack_diagonals(*means):
                    out_ref[own, at:at + value.shape[0]] = value.astype(NARROW)
                    at += value.shape[0]

    close, far = shaped(n, freqs, 2, 2, half, tile), shaped(freqs, length, tile)
    split = [shaped(count, length, tile) for count in (1, freqs - 1)]
    return pl.pallas_call(
        kernel,
        in_specs=[IN_SMEM, UNREAD] + [IN_VMEM] * 2,
        out_specs=[IN_VMEM] * (n + 1),
        out_shape=[close] * 2 + split + [far] * (n - 3),
        compiler_params=params(),
        cost_estimate=cost(0, 4 * moved.size),
    )(place, after, moved, pairs)


def scatter_rows(place, groups, pairs, n, after):
    tile = pairs.shape[-1]
    half = tile // 2
    counts = [rows[0].shape[1] for rows in groups]
    freqs = sum(counts)
    pair_at, diagonal_at, last_at, length = far_rows(n, tile)

    def kernel(place_ref, after_ref, *refs):
        pairs_ref, out_ref = refs[-2:]
        me = place_ref[0]
        mine = me % 2

        def put(block, d, f, c, value):
            value = value.astype(NARROW)
            at = (me ^ block) * 2
            out_ref[at, me ^ d, f, c] = value[:half]
            out_ref[at + 1, me ^ d, f, c] = value[half:]

        def put_all(row_refs, d, f, own):
            ref = row_refs[d]
            if d < 2:
                for block in range(n):
                    for c in range(2):
                        put(block, d, f, c, square(ref, block, own, c))
                return
            for block in range(2, n):
                for c in range(2):
                    put(block, d, f, c, ref[own, other_rows(block, c, tile)])
            put(1, d, f, mine, ref[own, pair_at:pair_at + tile])
            put(1, d, f, 1 - mine, pairs_ref[(d ^ 1) - 2, f].astype(WIDE).T)
            last = ref[own, last_at:length].astype(WIDE)
            for c in range(2):
                packed = ref[own, diagonal_at + c * half:diagonal_at + (c + 1) * half]
                put(0, d, f, c, unpack_diagonal(packed.astype(WIDE), last, c))

        f = 0
        for group, count in enumerate(counts):
            for own in range(count):
                for d in range(n):
                    put_all(refs[group * n:(group + 1) * n], d, f, own)
                f += 1

    arrays = [array for rows in groups for array in rows]
    return pl.pallas_call(
        kernel,
        in_specs=[IN_SMEM, UNREAD] + [IN_VMEM] * (len(arrays) + 1),
        out_specs=IN_VMEM,
        out_shape=shaped(2 * n, n, freqs, 2, half, tile),
        compiler_params=params(),
        cost_estimate=cost(0, 0),
    )(place, after, *arrays, pairs)


def side_by_side(parts, after):
    shape = parts[0].shape
    n = len(parts)

    def kernel(after_ref, *refs):
        for part, ref in enumerate(refs[:n]):
            refs[n][:, part] = ref[...]

    return pl.pallas_call(
        kernel,
        in_specs=[UNREAD] + [IN_VMEM] * n,
        out_specs=IN_VMEM,
        out_shape=shaped(shape[0], n, *shape[1:]),
        compiler_params=params(),
        cost_estimate=cost(0, 4 * n * parts[0].size),
    )(after, *parts)


def apart(moved, start):
    shape = moved.shape
    n, freqs = shape[1], shape[2] - start

    def kernel(moved_ref, *out_refs):
        for part, ref in enumerate(out_refs):
            ref[...] = moved_ref[:, part, start:]

    return pl.pallas_call(
        kernel,
        in_specs=[IN_VMEM],
        out_specs=[IN_VMEM] * n,
        out_shape=[shaped(shape[0], freqs, *shape[3:])] * n,
        compiler_params=params(),
        cost_estimate=cost(0, 0),
    )(moved)


def gate(value, *after):
    return lax.optimization_barrier((value, *after))[0]


def chunk_sizes(per_group):
    return [per_group // 2, per_group - per_group // 2]


def swapped(value, gap):
    size = lax.axis_size("src")
    return lax.ppermute(value, "src", [(i, i ^ gap) for i in range(size)])


def spread(value):
    return lax.all_to_all(value, "rcv", split_axis=0, concat_axis=0, tiled=True)


def local_tiles(records, surface_operator):
    src_tiles, rcv_tiles, samples = records.shape
    freqs = surface_operator.shape[0]
    n = lax.axis_size("src")
    devices = 2 * n * n
    half = src_tiles // 2
    me, column = lax.axis_index("src"), lax.axis_index("rcv")
    place = me.astype(jnp.int32)[None]
    sizes = chunk_sizes(freqs // devices)
    starts = [devices * sum(sizes[:q]) for q in range(len(sizes))]

    forward, inverse = host_tables(freqs, samples)

    def rows_of(table, q):
        return table[starts[q]:starts[q] + devices * sizes[q]]

    def by_owner(table, q):
        rows = rows_of(table, q).reshape(2 * n, n, sizes[q] * 2, samples)
        return rows.swapaxes(0, 1).reshape(n, -1, samples)

    coeffs = []
    for q, size in enumerate(sizes):
        at = starts[q] + (column * n + me) * size
        coeffs.append(lax.dynamic_slice_in_dim(surface_operator, at, size, 0))

    def first_part(q):
        if q == 0:
            return jnp.asarray(by_owner(forward, 0))
        return jnp.asarray(rows_of(forward, q).reshape(1, -1, samples))

    def over_src(rows):
        return [rows[0]] + [swapped(rows[d], d) for d in range(1, n)]

    def pair_of(moved, q):
        theirs = 1 - me % 2
        pairs = []
        for d in range(2, n):
            at = ((me ^ 1) * 2, me ^ d, 0, theirs, 0, 0)
            pair = lax.dynamic_slice(moved, at, (2, 1, sizes[q], 1, half, src_tiles))
            pairs.append(pair.reshape(2, sizes[q], half, src_tiles))
        return swapped(jnp.stack(pairs), 1)

    def spread_chunk(spectrum, q):
        return spread(spectrum.reshape(2 * n, n, sizes[q], 2, half, src_tiles))

    def gather(moved, q, after):
        return gather_rows(place, moved, pair_of(moved, q), n, after)

    def pairs_of(groups):
        pair_at = far_rows(n, src_tiles)[0]
        return jnp.stack(
            [
                jnp.concatenate([rows[d][:, pair_at:pair_at + src_tiles] for rows in groups])
                for d in range(2, n)
            ]
        )

    def flat(moved):
        return moved.reshape(-1, half, src_tiles)

    *early, spectrum = forward_dft(place, records, [first_part(0), first_part(1)], place)
    early = over_src(early)
    moved1 = spread_chunk(spectrum, 1)
    sent1 = gather(moved1, 1, place)
    first, others = (swapped(rows, 2) for rows in sent1[2:4])
    rows1 = [sent1[0], swapped(sent1[1], 1), first, others]
    rows1 += [swapped(sent1[d + 1], d) for d in range(3, n)]
    parts = [part.reshape(2 * n, sizes[0], 2, half, src_tiles) for part in early]
    moved0 = spread(gate(side_by_side(parts, sent1[0]), first))
    rest0 = predict(place, coeffs[0], [moved0], n, True, False, 1, sizes[0], sent1[0])
    sent0 = rest0[0]
    first0 = predict(place, coeffs[0], [moved0], n, True, False, 0, 1, sent0)
    sent0 = first0[0]
    first0 = over_src(first0)
    rest0 = over_src(rest0)
    back1 = predict(place, coeffs[1], rows1, n, False, True, 0, sizes[1], sent0)[0]
    moved = spread(gate(back1, *first0[1:]))
    first1 = over_src([moved[:, d, :1] for d in range(n)])
    rest1 = apart(moved, 1)
    sent1 = rest1[0]
    rest1 = over_src(rest1)
    pairs = swapped(pairs_of([first0, rest0]), 1)
    home0 = scatter_rows(place, [first0, rest0], pairs, n, sent1)
    home0 = spread(gate(home0, *first1[1:]))
    pieces = [[flat(home0)], [flat(x) for x in first1], [flat(x) for x in rest1]]
    last = by_owner(inverse, 1).reshape(n, 2 * n, sizes[1], 2, samples)
    tables = [
        jnp.asarray(rows_of(inverse, 0).reshape(1, -1, samples)),
        jnp.asarray(last[:, :, :1].reshape(n, -1, samples)),
        jnp.asarray(last[:, :, 1:].reshape(n, -1, samples)),
    ]
    return inverse_dft(place, pieces, tables)


def solution(mesh):
    placed = (P("src", "rcv", None), P())
    n_src, n_rcv = mesh.shape["src"], mesh.shape["rcv"]

    def local(records, surface_operator):
        src_tiles, rcv_tiles, _ = records.shape
        per_group = surface_operator.shape[0] // (n_src * n_rcv)
        square_tiles = n_rcv == 2 * n_src and src_tiles == 2 * rcv_tiles
        whole_lanes = src_tiles % 128 == 0 and n_src >= 4 and n_src & (n_src - 1) == 0
        if square_tiles and whole_lanes and per_group >= 4:
            return local_tiles(records, surface_operator)
        return local_general(records, surface_operator)

    return jax.shard_map(
        local, mesh=mesh, in_specs=placed, out_specs=P("src", "rcv", None), check_vma=False
    )
```

```python
import math

import jax
import jax.numpy as jnp
from jax import lax
from jax.sharding import PartitionSpec as P
from jax.experimental import pallas as pl
from jax.experimental.pallas import tpu as pltpu
import ml_dtypes
import numpy as np


def dft_tables(freqs, samples):
    freq_index = lax.broadcasted_iota(jnp.int32, (freqs, samples), 0)
    time_index = lax.broadcasted_iota(jnp.int32, (freqs, samples), 1)
    phase = (freq_index * time_index % samples).astype(jnp.float32)
    angle = phase * (2.0 * math.pi / samples)
    norming = 1.0 / math.sqrt(samples)
    cosine = jnp.cos(angle) * norming
    sine = jnp.sin(angle) * norming
    weights = jnp.where(freq_index == 0, 1.0, 2.0).astype(jnp.float32)
    forward = jnp.stack([cosine, -sine], axis=1).reshape(2 * freqs, samples)
    inverse = jnp.stack([weights * cosine, -weights * sine], axis=1).reshape(2 * freqs, samples)
    return (forward.astype(jnp.bfloat16), inverse.astype(jnp.bfloat16))


def batch_product(left, right):

    def mult(first_op, second_op):
        return jnp.einsum("nij,njk->nik", first_op, second_op, preferred_element_type=jnp.float32)

    real_part = mult(left[:, 0], right[:, 0]) - mult(left[:, 1], right[:, 1])
    imag_part = mult(left[:, 0], right[:, 1]) + mult(left[:, 1], right[:, 0])
    return (real_part, imag_part)


def predict_block(blocks, coeff):
    order = blocks.shape[2]
    recip = (
        0.5 * (blocks.astype(jnp.float32) + jnp.swapaxes(blocks, 2, 3).astype(jnp.float32))
    ).astype(jnp.bfloat16)
    factor = coeff / math.sqrt(order)
    real_k = factor[:, 0][:, None, None]
    imag_k = factor[:, 1][:, None, None]

    def scaled(product):
        return jnp.stack(
            [real_k * product[0] - imag_k * product[1], real_k * product[1] + imag_k * product[0]],
            axis=1,
        )

    first = scaled(batch_product(recip, recip)).astype(jnp.bfloat16)
    second = scaled(batch_product(recip, first)).astype(jnp.bfloat16)
    third = scaled(batch_product(recip, second))
    return (first.astype(jnp.float32) + second.astype(jnp.float32) + third).astype(jnp.bfloat16)


def local_general(records, surface_operator):
    src_tiles, rcv_tiles, samples = records.shape
    freqs = surface_operator.shape[0]
    n_src = lax.axis_size("src")
    n_rcv = lax.axis_size("rcv")
    per_group = freqs // (n_src * n_rcv)
    columns = src_tiles * rcv_tiles
    whole_src = n_src * src_tiles
    whole_rcv = n_rcv * rcv_tiles
    forward, inverse = dft_tables(freqs, samples)
    flat_traces = records.reshape(columns, samples)
    spectrum = jnp.einsum(
        "kt,nt->kn", forward, flat_traces, preferred_element_type=jnp.float32
    ).astype(jnp.bfloat16)
    group_index = lax.axis_index("src") * n_rcv + lax.axis_index("rcv")
    coeff = lax.dynamic_slice_in_dim(surface_operator, group_index * per_group, per_group, 0)
    moved = lax.all_to_all(
        spectrum.reshape(freqs, 2, 1, columns),
        ("src", "rcv"),
        split_axis=0,
        concat_axis=2,
        tiled=True,
    )
    blocks = moved.reshape(per_group, 2, n_src, n_rcv, src_tiles, rcv_tiles)
    blocks = blocks.transpose(0, 1, 2, 4, 3, 5).reshape(per_group, 2, whole_src, whole_rcv)
    predicted = predict_block(blocks, coeff)
    outgoing = predicted.reshape(per_group, 2, n_src, src_tiles, n_rcv, rcv_tiles).transpose(
        0, 1, 2, 4, 3, 5
    )
    returned = lax.all_to_all(
        outgoing.reshape(1, per_group, 2, n_src * n_rcv, columns),
        ("src", "rcv"),
        split_axis=3,
        concat_axis=0,
        tiled=True,
    )
    returned = returned.reshape(2 * freqs, columns)
    result = jnp.einsum("kn,kt->nt", returned, inverse, preferred_element_type=jnp.float32)
    return result.astype(jnp.bfloat16).reshape(src_tiles, rcv_tiles, samples)


NT = (((1,), (1,)), ((), ()))
TN = (((0,), (0,)), ((), ()))
VMEM_LIMIT = 56 * 2**20
ROWS = 16
BATCH = 4
WIDE = jnp.float32
NARROW = jnp.bfloat16
IN_VMEM = pl.BlockSpec(memory_space=pltpu.VMEM)
IN_SMEM = pl.BlockSpec(memory_space=pltpu.SMEM)
UNREAD = pl.BlockSpec(memory_space=pl.ANY)


def host_tables(freqs, samples):
    f = np.arange(freqs)[:, None]
    t = np.arange(samples)[None, :]
    angle = (f * t % samples) * (2.0 * math.pi / samples)
    norming = 1.0 / math.sqrt(samples)
    cosine = np.cos(angle) * norming
    sine = np.sin(angle) * norming
    weights = np.where(f == 0, 1.0, 2.0)
    forward = np.stack([cosine, -sine], axis=1)
    inverse = np.stack([weights * cosine, -weights * sine], axis=1)
    return [x.astype(np.float32).astype(ml_dtypes.bfloat16) for x in (forward, inverse)]


def params():
    return pltpu.CompilerParams(vmem_limit_bytes=VMEM_LIMIT)


def cost(flops, moved):
    return pl.CostEstimate(flops=0, bytes_accessed=0, transcendentals=0)


def shaped(*shape):
    return jax.ShapeDtypeStruct(shape, NARROW)


def forward_dft(place, records, tables, after):
    sources, receivers, samples = records.shape
    half = sources // 2
    width = 2 * receivers
    sizes = [table.shape[1] for table in tables for _ in range(table.shape[0])]
    rows = sum(sizes)

    def kernel(place_ref, after_ref, *refs):
        table_refs, records_ref = refs[:len(tables)], refs[len(tables)]
        out_refs, (turned, table) = refs[len(tables) + 1:-2], refs[-2:]

        @pl.when(pl.program_id(0) == 0)
        def _():
            at = 0
            for ref in table_refs:
                parts, size, _ = ref.shape
                for part in range(parts):
                    which = (place_ref[0] ^ part) if parts > 1 else 0
                    table[at:at + size, :] = ref[which]
                    at += size

        for p in range(0, ROWS, 2):
            traces = jnp.concatenate(
                [records_ref[s, p + d] for d in range(2) for s in range(2)], axis=0
            )
            found = lax.dot_general(table[...], traces, NT, preferred_element_type=WIDE)
            found = found.astype(NARROW)
            turned[p] = found[:, :width]
            turned[p + 1] = found[:, width:]
        at = 0
        for out_ref, size in zip(out_refs, sizes):
            out_ref[...] = jnp.swapaxes(turned[:, at:at + size, :], 0, 1)
            at += size

    return pl.pallas_call(
        kernel,
        grid=(half // ROWS,),
        in_specs=[IN_SMEM, UNREAD]
        + [pl.BlockSpec(table.shape, lambda i: (0, 0, 0)) for table in tables]
        + [pl.BlockSpec((2, ROWS, receivers, samples), lambda i: (0, i, 0, 0))],
        out_specs=[pl.BlockSpec((size, ROWS, width), lambda i: (0, i, 0)) for size in sizes],
        out_shape=[shaped(size, half, width) for size in sizes],
        scratch_shapes=[
            pltpu.VMEM((ROWS, rows, width), NARROW),
            pltpu.VMEM((rows, samples), NARROW),
        ],
        compiler_params=params(),
        cost_estimate=cost(2 * rows * records.size, 2 * (records.size + rows * half * width)),
    )(place, after, *tables, records.reshape(2, half, receivers, samples))


def inverse_dft(place, pieces, tables):
    half, width = pieces[0][0].shape[1:]
    receivers = width // 2
    samples = tables[0].shape[-1]
    spectra = [piece for group in pieces for piece in group]
    sizes = [piece.shape[0] for piece in spectra]
    rows = sum(sizes)

    def kernel(place_ref, *refs):
        table_refs = refs[:len(tables)]
        spectra_refs = refs[len(tables):len(tables) + len(spectra)]
        out_ref, turned, table = refs[len(tables) + len(spectra):]

        @pl.when(pl.program_id(0) == 0)
        def _():
            at = 0
            for table_ref, group in zip(table_refs, pieces):
                for part, piece in enumerate(group):
                    size = piece.shape[0]
                    which = (place_ref[0] ^ part) if len(group) > 1 else 0
                    table[at:at + size, :] = table_ref[which]
                    at += size

        at = 0
        for ref, size in zip(spectra_refs, sizes):
            turned[:, at:at + size, :] = jnp.swapaxes(ref[...], 0, 1)
            at += size
        for p in range(0, ROWS, BATCH):
            columns = [turned[p + q] for q in range(BATCH)]
            traces = lax.dot_general(
                jnp.concatenate(columns, axis=1), table[...], TN, preferred_element_type=WIDE
            ).astype(out_ref.dtype)
            for q in range(BATCH):
                out_ref[0, p + q] = traces[q * width:q * width + receivers]
                out_ref[1, p + q] = traces[q * width + receivers:(q + 1) * width]

    return pl.pallas_call(
        kernel,
        grid=(half // ROWS,),
        in_specs=[IN_SMEM]
        + [pl.BlockSpec(table.shape, lambda i: (0, 0, 0)) for table in tables]
        + [pl.BlockSpec((size, ROWS, width), lambda i: (0, i, 0)) for size in sizes],
        out_specs=pl.BlockSpec((2, ROWS, receivers, samples), lambda i: (0, i, 0, 0)),
        out_shape=shaped(2, half, receivers, samples),
        scratch_shapes=[
            pltpu.VMEM((ROWS, rows, width), NARROW),
            pltpu.VMEM((rows, samples), NARROW),
        ],
        compiler_params=params(),
        cost_estimate=cost(
            2 * rows * half * width * samples, 2 * half * width * (samples + rows)
        ),
    )(place, *tables, *spectra).reshape(2 * half, receivers, samples)


def swap_quarters(block):
    half = block.shape[0] // 2
    return jnp.concatenate(
        [
            jnp.concatenate([block[:half, :half], block[half:, :half]], axis=1),
            jnp.concatenate([block[:half, half:], block[half:, half:]], axis=1),
        ],
        axis=0,
    )


def left_half(rows, lanes):
    return lax.broadcasted_iota(jnp.int32, (rows, lanes), 1) < lanes // 2


def places(half):
    shape = (half, 2 * half)
    rows = lax.broadcasted_iota(jnp.int32, shape, 0)
    lanes = lax.broadcasted_iota(jnp.int32, shape, 1)
    left = lanes < half
    return rows, jnp.where(left, lanes, lanes - half), left


def pack_diagonals(real, imag):
    half = real.shape[0] // 2
    rows, lanes, left = places(half)
    packed, diagonals = [], []
    for block in (real, imag):
        lower = pltpu.roll(block[half:], half, 1)
        packed.append(jnp.where(left & (rows > lanes), lower, block[:half]))
        diagonals.append(jnp.where(rows == lanes, block[half:], 0.0))
    both = jnp.where(left, pltpu.roll(diagonals[0], half, 1), diagonals[1])
    both = jnp.sum(both, axis=0, keepdims=True)
    return packed[0], packed[1], jnp.broadcast_to(both, (ROWS, 2 * half))


def unpack_diagonal(packed, diagonals, c):
    half, size = packed.shape
    rows, lanes, left = places(half)
    mirrored = jnp.concatenate([packed, packed], axis=0).T
    diagonal = diagonals[:1]
    if c == 0:
        diagonal = pltpu.roll(jnp.broadcast_to(diagonal, (8, size)), half, 1)[:1]
    top = jnp.where(left & (rows > lanes), mirrored[:half], packed)
    last = jnp.where(rows > lanes, pltpu.roll(packed, half, 1), mirrored[:half])
    last = jnp.where(rows == lanes, diagonal, last)
    return jnp.concatenate([top, jnp.where(left, mirrored[half:], last)], axis=0)


def square(ref, *at):
    halves = ref[at] if at else ref[...]
    return halves.astype(WIDE).reshape(2 * halves.shape[-2], halves.shape[-1])


def dot(left, right):
    return jnp.dot(left, right, preferred_element_type=WIDE)


def series(real_k, imag_k, recip, first, out_block, tile):
    order = recip.shape[-1]
    panel = min(2 * tile, order)

    def scaled(real, imag):
        return real_k * real - imag_k * imag, real_k * imag + imag_k * real

    for start in range(0, order, panel):
        rows = pl.ds(start, panel)
        a, b = recip[0, rows, :], recip[1, rows, :]
        real, imag = scaled(
            dot(a, recip[0]) - dot(b, recip[1]), dot(a, recip[1]) + dot(b, recip[0])
        )
        first[0, rows, :] = real.astype(NARROW)
        first[1, rows, :] = imag.astype(NARROW)
    for start in range(0, order, panel):
        rows = pl.ds(start, panel)
        own = [first[c, rows, :].astype(WIDE) for c in range(2)]
        a, b = [(recip[c, rows, :].astype(WIDE) + own[c]).astype(NARROW) for c in range(2)]
        real, imag = scaled(
            dot(a, first[0]) - dot(b, first[1]), dot(a, first[1]) + dot(b, first[0])
        )
        real, imag = own[0] + real, own[1] + imag
        for row in range(0, panel, tile):
            for b in range(order // tile):
                at = (slice(row, row + tile), slice(b * tile, (b + 1) * tile))
                out_block(
                    (start + row) // tile, b, swap_quarters(real[at].astype(NARROW)), swap_quarters(imag[at].astype(NARROW))
                )


def far_rows(n, tile):
    pair = 2 * (n - 2) * tile
    return pair, pair + tile, pair + 2 * tile, pair + 2 * tile + ROWS


def other_rows(block, c, tile):
    at = (2 * (block - 2) + c) * tile
    return slice(at, at + tile)


def predict(place, coeff, moved, n, direct_in, direct_out, start, stop, after):
    freqs = stop - start
    half, tile = moved[0].shape[-2:]
    order = n * tile
    pair_at, diagonal_at, last_at, length = far_rows(n, tile)

    def kernel(place_ref, coeff_ref, after_ref, *refs):
        count = 1 if direct_in else n + 1
        moved_refs, refs = refs[:count], refs[count:]
        ahead = pl.program_id(0) == 0

        def far(i, rows):
            if i > 2:
                return moved_refs[i + 1][0, rows].astype(WIDE)
            one, other = (moved_refs[k][0, rows].astype(WIDE) for k in (2, 3))
            return jnp.where(ahead, one, other)

        count = 1 if direct_out else n
        out_refs, (recip, first) = refs[:count], refs[count:]
        me = place_ref[0]
        odd = me % 2 == 1

        def stacked(c, i, j):
            if direct_in:
                return square(moved_refs[0], pl.ds((j ^ me) * 2, 2), i, 0, c)
            if i < 2:
                return square(moved_refs[i], i ^ j, 0, c)
            return far(i, other_rows(i ^ j, c, tile))

        def mean(c, a, b):
            if direct_in or a < 2 or (a ^ b) >= 2:
                turned = stacked(c, b, a).astype(NARROW).T.astype(WIDE)
                return 0.5 * (stacked(c, a, b) + turned)
            if a == b:
                at = diagonal_at + c * half
                packed = far(a, slice(at, at + half))
                return unpack_diagonal(packed, far(a, slice(last_at, length)), c)
            here = far(a, slice(pair_at, pair_at + tile))
            there = far(b, slice(pair_at, pair_at + tile)).T
            return jnp.where(odd == (c == 0), here, there)

        for c in range(2):
            for a in range(n):
                for b in range(a + 1):
                    block = swap_quarters(mean(c, a, b).astype(NARROW))
                    rows, columns = slice(a * tile, (a + 1) * tile), slice(b * tile, (b + 1) * tile)
                    recip[c, rows, columns] = block.astype(NARROW)
                    if a != b:
                        recip[c, columns, rows] = block.astype(NARROW).T

        def out_block(a, b, real, imag):
            gap = a ^ b
            if not direct_out and a >= 2 and gap == 1:
                own = jnp.where(odd == (a % 2 == 0), imag, real).astype(NARROW)
                out_refs[a][0, pair_at:pair_at + tile] = own
                return
            if not direct_out and a >= 2 and gap == 0:
                at = diagonal_at
                for value in pack_diagonals(real.astype(WIDE), imag.astype(WIDE)):
                    out_refs[a][0, at:at + value.shape[0]] = value.astype(NARROW)
                    at += value.shape[0]
                return
            for c, value in enumerate((real, imag)):
                value = value.astype(NARROW)
                if not direct_out and a >= 2:
                    out_refs[a][0, other_rows(gap, c, tile)] = value
                    continue
                for h in range(2):
                    part = value[h * half:(h + 1) * half]
                    if direct_out:
                        out_refs[0][(b ^ me) * 2 + h, a, 0, c] = part
                    else:
                        out_refs[a][gap, 0, c, h] = part

        index = pl.program_id(0) + start
        series(coeff_ref[index, 0], coeff_ref[index, 1], recip, first, out_block, tile)

    whole = (2 * n, n, freqs, 2, half, tile)
    close = (n, freqs, 2, 2, half, tile)
    far = (freqs, length, tile)
    split_shapes = [shaped(*close)] * 2 + [shaped(*far)] * (n - 2)

    def specs(direct, first, split):
        if direct:
            block = (2 * n, n, 1, 2, half, tile)
            return [pl.BlockSpec(block, lambda i: (0, 0, i + first, 0, 0, 0))]
        close = pl.BlockSpec((n, 1, 2, 2, half, tile), lambda i: (0, i + first, 0, 0, 0, 0))
        far = pl.BlockSpec((1, length, tile), lambda i: (i + first, 0, 0))
        if not split:
            return [close] * 2 + [far] * (n - 2)
        one = pl.BlockSpec((1, length, tile), lambda i: (0, 0, 0))
        others = pl.BlockSpec((1, length, tile), lambda i: (jnp.maximum(i - 1, 0), 0, 0))
        return [close] * 2 + [one, others] + [far] * (n - 3)

    return pl.pallas_call(
        kernel,
        grid=(freqs,),
        in_specs=[IN_SMEM, IN_SMEM, UNREAD] + specs(direct_in, start, True),
        out_specs=specs(direct_out, 0, False),
        out_shape=[shaped(*whole)] if direct_out else split_shapes,
        scratch_shapes=[pltpu.VMEM((2, order, order), NARROW)] * 2,
        compiler_params=params(),
        cost_estimate=cost(16 * freqs * order**3, 16 * freqs * order**2),
    )(place, coeff / math.sqrt(order), after, *moved)


def gather_rows(place, moved, pairs, n, after):
    _, _, freqs, _, half, tile = moved.shape
    pair_at, diagonal_at, last_at, length = far_rows(n, tile)

    def kernel(place_ref, after_ref, moved_ref, pairs_ref, *out_refs):
        me = place_ref[0]
        mine = me % 2

        def halves(block):
            return pl.ds((me ^ block) * 2, 2)

        for d in range(2):
            for block in range(n):
                for f in range(freqs):
                    for c in range(2):
                        out_refs[d][block, f, c] = moved_ref[halves(block), me ^ d, f, c]
        for d in range(2, n):
            for f in range(freqs):
                out_ref, own = (out_refs[d + 1], f) if d > 2 or f else (out_refs[2], 0)
                own = f - 1 if d == 2 and f else own
                for block in range(2, n):
                    for c in range(2):
                        rows = moved_ref[halves(block), me ^ d, f, c].reshape(tile, tile)
                        out_ref[own, other_rows(block, c, tile)] = rows
                here = square(moved_ref, halves(1), me ^ d, f, mine)
                there = square(pairs_ref, (d ^ 1) - 2, slice(None), f)
                mean = (0.5 * (here + there.T)).astype(NARROW)
                out_ref[own, pair_at:pair_at + tile] = mean
                means = []
                for c in range(2):
                    block = square(moved_ref, halves(0), me ^ d, f, c)
                    means.append(0.5 * (block + block.T))
                at = diagonal_at
                for value in pack_diagonals(*means):
                    out_ref[own, at:at + value.shape[0]] = value.astype(NARROW)
                    at += value.shape[0]

    close, far = shaped(n, freqs, 2, 2, half, tile), shaped(freqs, length, tile)
    split = [shaped(count, length, tile) for count in (1, freqs - 1)]
    return pl.pallas_call(
        kernel,
        in_specs=[IN_SMEM, UNREAD] + [IN_VMEM] * 2,
        out_specs=[IN_VMEM] * (n + 1),
        out_shape=[close] * 2 + split + [far] * (n - 3),
        compiler_params=params(),
        cost_estimate=cost(0, 4 * moved.size),
    )(place, after, moved, pairs)


def scatter_rows(place, groups, pairs, n, after):
    tile = pairs.shape[-1]
    half = tile // 2
    counts = [rows[0].shape[1] for rows in groups]
    freqs = sum(counts)
    pair_at, diagonal_at, last_at, length = far_rows(n, tile)

    def kernel(place_ref, after_ref, *refs):
        pairs_ref, out_ref = refs[-2:]
        me = place_ref[0]
        mine = me % 2

        def put(block, d, f, c, value):
            value = value.astype(NARROW)
            at = (me ^ block) * 2
            out_ref[at, me ^ d, f, c] = value[:half]
            out_ref[at + 1, me ^ d, f, c] = value[half:]

        def put_all(row_refs, d, f, own):
            ref = row_refs[d]
            if d < 2:
                for block in range(n):
                    for c in range(2):
                        put(block, d, f, c, square(ref, block, own, c))
                return
            for block in range(2, n):
                for c in range(2):
                    put(block, d, f, c, ref[own, other_rows(block, c, tile)])
            put(1, d, f, mine, ref[own, pair_at:pair_at + tile])
            put(1, d, f, 1 - mine, pairs_ref[(d ^ 1) - 2, f].astype(WIDE).T)
            last = ref[own, last_at:length].astype(WIDE)
            for c in range(2):
                packed = ref[own, diagonal_at + c * half:diagonal_at + (c + 1) * half]
                put(0, d, f, c, unpack_diagonal(packed.astype(WIDE), last, c))

        f = 0
        for group, count in enumerate(counts):
            for own in range(count):
                for d in range(n):
                    put_all(refs[group * n:(group + 1) * n], d, f, own)
                f += 1

    arrays = [array for rows in groups for array in rows]
    return pl.pallas_call(
        kernel,
        in_specs=[IN_SMEM, UNREAD] + [IN_VMEM] * (len(arrays) + 1),
        out_specs=IN_VMEM,
        out_shape=shaped(2 * n, n, freqs, 2, half, tile),
        compiler_params=params(),
        cost_estimate=cost(0, 0),
    )(place, after, *arrays, pairs)


def apart(moved, start):
    shape = moved.shape
    n, freqs = shape[1], shape[2] - start

    def kernel(moved_ref, *out_refs):
        for part, ref in enumerate(out_refs):
            ref[...] = moved_ref[:, part, start:]

    return pl.pallas_call(
        kernel,
        in_specs=[IN_VMEM],
        out_specs=[IN_VMEM] * n,
        out_shape=[shaped(shape[0], freqs, *shape[3:])] * n,
        compiler_params=params(),
        cost_estimate=cost(0, 0),
    )(moved)


def gate(value, *after):
    return lax.optimization_barrier((value, *after))[0]


def chunk_sizes(per_group):
    return [per_group // 2, per_group - per_group // 2]


def swapped(value, gap):
    size = lax.axis_size("src")
    return lax.ppermute(value, "src", [(i, i ^ gap) for i in range(size)])


def spread(value):
    return lax.all_to_all(value, "rcv", split_axis=0, concat_axis=0, tiled=True)


def local_tiles(records, surface_operator):
    src_tiles, rcv_tiles, samples = records.shape
    freqs = surface_operator.shape[0]
    n = lax.axis_size("src")
    devices = 2 * n * n
    half = src_tiles // 2
    me, column = lax.axis_index("src"), lax.axis_index("rcv")
    place = me.astype(jnp.int32)[None]
    sizes = chunk_sizes(freqs // devices)
    starts = [devices * sum(sizes[:q]) for q in range(len(sizes))]

    forward, inverse = host_tables(freqs, samples)

    def rows_of(table, q):
        return table[starts[q]:starts[q] + devices * sizes[q]]

    def by_owner(table, q):
        rows = rows_of(table, q).reshape(2 * n, n, sizes[q] * 2, samples)
        return rows.swapaxes(0, 1).reshape(n, -1, samples)

    coeffs = []
    for q, size in enumerate(sizes):
        at = starts[q] + (column * n + me) * size
        coeffs.append(lax.dynamic_slice_in_dim(surface_operator, at, size, 0))

    def first_part(q):
        if q == 0:
            return jnp.asarray(by_owner(forward, 0))
        return jnp.asarray(rows_of(forward, q).reshape(1, -1, samples))

    def over_src(rows):
        return [rows[0]] + [swapped(rows[d], d) for d in range(1, n)]

    def pair_of(moved, q):
        theirs = 1 - me % 2
        pairs = []
        for d in range(2, n):
            at = ((me ^ 1) * 2, me ^ d, 0, theirs, 0, 0)
            pair = lax.dynamic_slice(moved, at, (2, 1, sizes[q], 1, half, src_tiles))
            pairs.append(pair.reshape(2, sizes[q], half, src_tiles))
        return swapped(jnp.stack(pairs), 1)

    def spread_chunk(spectrum, q):
        return spread(spectrum.reshape(2 * n, n, sizes[q], 2, half, src_tiles))

    def gather(moved, q, after):
        return gather_rows(place, moved, pair_of(moved, q), n, after)

    def pairs_of(groups):
        pair_at = far_rows(n, src_tiles)[0]
        return jnp.stack(
            [
                jnp.concatenate([rows[d][:, pair_at:pair_at + src_tiles] for rows in groups])
                for d in range(2, n)
            ]
        )

    def flat(moved):
        return moved.reshape(-1, half, src_tiles)

    *early, spectrum = forward_dft(place, records, [first_part(0), first_part(1)], place)
    early = over_src(early)
    moved1 = spread_chunk(spectrum, 1)
    sent1 = gather(moved1, 1, place)
    first, others = (swapped(rows, 2) for rows in sent1[2:4])
    rows1 = [sent1[0], swapped(sent1[1], 1), first, others]
    rows1 += [swapped(sent1[d + 1], d) for d in range(3, n)]
    parts = [part.reshape(2 * n, 1, sizes[0], 2, half, src_tiles) for part in early]
    joined = jnp.concatenate([gate(part, sent1[0], first) for part in parts], axis=1)
    moved0 = spread(joined)
    rest0 = predict(place, coeffs[0], [moved0], n, True, False, 1, sizes[0], sent1[0])
    sent0 = rest0[0]
    first0 = predict(place, coeffs[0], [moved0], n, True, False, 0, 1, sent0)
    sent0 = first0[0]
    first0 = over_src(first0)
    rest0 = over_src(rest0)
    back1 = predict(place, coeffs[1], rows1, n, False, True, 0, sizes[1], sent0)[0]
    moved = spread(gate(back1, *first0[1:]))
    first1 = over_src([moved[:, d, :1] for d in range(n)])
    rest1 = apart(moved, 1)
    sent1 = rest1[0]
    rest1 = over_src(rest1)
    pairs = swapped(pairs_of([first0, rest0]), 1)
    home0 = scatter_rows(place, [first0, rest0], pairs, n, sent1)
    home0 = spread(gate(home0, *first1[1:]))
    pieces = [[flat(home0)], [flat(x) for x in first1], [flat(x) for x in rest1]]
    last = by_owner(inverse, 1).reshape(n, 2 * n, sizes[1], 2, samples)
    tables = [
        jnp.asarray(rows_of(inverse, 0).reshape(1, -1, samples)),
        jnp.asarray(last[:, :, :1].reshape(n, -1, samples)),
        jnp.asarray(last[:, :, 1:].reshape(n, -1, samples)),
    ]
    return inverse_dft(place, pieces, tables)


def solution(mesh):
    placed = (P("src", "rcv", None), P())
    n_src, n_rcv = mesh.shape["src"], mesh.shape["rcv"]

    def local(records, surface_operator):
        src_tiles, rcv_tiles, _ = records.shape
        per_group = surface_operator.shape[0] // (n_src * n_rcv)
        square_tiles = n_rcv == 2 * n_src and src_tiles == 2 * rcv_tiles
        whole_lanes = src_tiles % 128 == 0 and n_src >= 4 and n_src & (n_src - 1) == 0
        if square_tiles and whole_lanes and per_group >= 4:
            return local_tiles(records, surface_operator)
        return local_general(records, surface_operator)

    return jax.shard_map(
        local, mesh=mesh, in_specs=placed, out_specs=P("src", "rcv", None), check_vma=False
    )
```

```python
import math

import jax
import jax.numpy as jnp
from jax import lax
from jax.sharding import PartitionSpec as P
from jax.experimental import pallas as pl
from jax.experimental.pallas import tpu as pltpu
import ml_dtypes
import numpy as np


def dft_tables(freqs, samples):
    freq_index = lax.broadcasted_iota(jnp.int32, (freqs, samples), 0)
    time_index = lax.broadcasted_iota(jnp.int32, (freqs, samples), 1)
    phase = (freq_index * time_index % samples).astype(jnp.float32)
    angle = phase * (2.0 * math.pi / samples)
    norming = 1.0 / math.sqrt(samples)
    cosine = jnp.cos(angle) * norming
    sine = jnp.sin(angle) * norming
    weights = jnp.where(freq_index == 0, 1.0, 2.0).astype(jnp.float32)
    forward = jnp.stack([cosine, -sine], axis=1).reshape(2 * freqs, samples)
    inverse = jnp.stack([weights * cosine, -weights * sine], axis=1).reshape(2 * freqs, samples)
    return (forward.astype(jnp.bfloat16), inverse.astype(jnp.bfloat16))


def batch_product(left, right):

    def mult(first_op, second_op):
        return jnp.einsum("nij,njk->nik", first_op, second_op, preferred_element_type=jnp.float32)

    real_part = mult(left[:, 0], right[:, 0]) - mult(left[:, 1], right[:, 1])
    imag_part = mult(left[:, 0], right[:, 1]) + mult(left[:, 1], right[:, 0])
    return (real_part, imag_part)


def predict_block(blocks, coeff):
    order = blocks.shape[2]
    recip = (
        0.5 * (blocks.astype(jnp.float32) + jnp.swapaxes(blocks, 2, 3).astype(jnp.float32))
    ).astype(jnp.bfloat16)
    factor = coeff / math.sqrt(order)
    real_k = factor[:, 0][:, None, None]
    imag_k = factor[:, 1][:, None, None]

    def scaled(product):
        return jnp.stack(
            [real_k * product[0] - imag_k * product[1], real_k * product[1] + imag_k * product[0]],
            axis=1,
        )

    first = scaled(batch_product(recip, recip)).astype(jnp.bfloat16)
    second = scaled(batch_product(recip, first)).astype(jnp.bfloat16)
    third = scaled(batch_product(recip, second))
    return (first.astype(jnp.float32) + second.astype(jnp.float32) + third).astype(jnp.bfloat16)


def local_general(records, surface_operator):
    src_tiles, rcv_tiles, samples = records.shape
    freqs = surface_operator.shape[0]
    n_src = lax.axis_size("src")
    n_rcv = lax.axis_size("rcv")
    per_group = freqs // (n_src * n_rcv)
    columns = src_tiles * rcv_tiles
    whole_src = n_src * src_tiles
    whole_rcv = n_rcv * rcv_tiles
    forward, inverse = dft_tables(freqs, samples)
    flat_traces = records.reshape(columns, samples)
    spectrum = jnp.einsum(
        "kt,nt->kn", forward, flat_traces, preferred_element_type=jnp.float32
    ).astype(jnp.bfloat16)
    group_index = lax.axis_index("src") * n_rcv + lax.axis_index("rcv")
    coeff = lax.dynamic_slice_in_dim(surface_operator, group_index * per_group, per_group, 0)
    moved = lax.all_to_all(
        spectrum.reshape(freqs, 2, 1, columns),
        ("src", "rcv"),
        split_axis=0,
        concat_axis=2,
        tiled=True,
    )
    blocks = moved.reshape(per_group, 2, n_src, n_rcv, src_tiles, rcv_tiles)
    blocks = blocks.transpose(0, 1, 2, 4, 3, 5).reshape(per_group, 2, whole_src, whole_rcv)
    predicted = predict_block(blocks, coeff)
    outgoing = predicted.reshape(per_group, 2, n_src, src_tiles, n_rcv, rcv_tiles).transpose(
        0, 1, 2, 4, 3, 5
    )
    returned = lax.all_to_all(
        outgoing.reshape(1, per_group, 2, n_src * n_rcv, columns),
        ("src", "rcv"),
        split_axis=3,
        concat_axis=0,
        tiled=True,
    )
    returned = returned.reshape(2 * freqs, columns)
    result = jnp.einsum("kn,kt->nt", returned, inverse, preferred_element_type=jnp.float32)
    return result.astype(jnp.bfloat16).reshape(src_tiles, rcv_tiles, samples)


NT = (((1,), (1,)), ((), ()))
TN = (((0,), (0,)), ((), ()))
VMEM_LIMIT = 56 * 2**20
ROWS = 16
BATCH = 4
WIDE = jnp.float32
NARROW = jnp.bfloat16
IN_VMEM = pl.BlockSpec(memory_space=pltpu.VMEM)
IN_SMEM = pl.BlockSpec(memory_space=pltpu.SMEM)
UNREAD = pl.BlockSpec(memory_space=pl.ANY)


def host_tables(freqs, samples):
    f = np.arange(freqs)[:, None]
    t = np.arange(samples)[None, :]
    angle = (f * t % samples) * (2.0 * math.pi / samples)
    norming = 1.0 / math.sqrt(samples)
    cosine = np.cos(angle) * norming
    sine = np.sin(angle) * norming
    weights = np.where(f == 0, 1.0, 2.0)
    forward = np.stack([cosine, -sine], axis=1)
    inverse = np.stack([weights * cosine, -weights * sine], axis=1)
    return [x.astype(np.float32).astype(ml_dtypes.bfloat16) for x in (forward, inverse)]


def params():
    return pltpu.CompilerParams(vmem_limit_bytes=VMEM_LIMIT)


def cost(flops, moved):
    return pl.CostEstimate(flops=0, bytes_accessed=0, transcendentals=0)


def shaped(*shape):
    return jax.ShapeDtypeStruct(shape, NARROW)


def forward_dft(place, records, tables, after):
    sources, receivers, samples = records.shape
    half = sources // 2
    width = 2 * receivers
    sizes = [table.shape[1] for table in tables for _ in range(table.shape[0])]
    rows = sum(sizes)

    def kernel(place_ref, after_ref, *refs):
        table_refs, records_ref = refs[:len(tables)], refs[len(tables)]
        out_refs, (turned, table) = refs[len(tables) + 1:-2], refs[-2:]

        @pl.when(pl.program_id(0) == 0)
        def _():
            at = 0
            for ref in table_refs:
                parts, size, _ = ref.shape
                for part in range(parts):
                    which = (place_ref[0] ^ part) if parts > 1 else 0
                    table[at:at + size, :] = ref[which]
                    at += size

        for p in range(0, ROWS, 2):
            traces = jnp.concatenate(
                [records_ref[s, p + d] for d in range(2) for s in range(2)], axis=0
            )
            found = lax.dot_general(table[...], traces, NT, preferred_element_type=WIDE)
            found = found.astype(NARROW)
            turned[p] = found[:, :width]
            turned[p + 1] = found[:, width:]
        at = 0
        for out_ref, size in zip(out_refs, sizes):
            out_ref[...] = jnp.swapaxes(turned[:, at:at + size, :], 0, 1)
            at += size

    return pl.pallas_call(
        kernel,
        grid=(half // ROWS,),
        in_specs=[IN_SMEM, UNREAD]
        + [pl.BlockSpec(table.shape, lambda i: (0, 0, 0)) for table in tables]
        + [pl.BlockSpec((2, ROWS, receivers, samples), lambda i: (0, i, 0, 0))],
        out_specs=[pl.BlockSpec((size, ROWS, width), lambda i: (0, i, 0)) for size in sizes],
        out_shape=[shaped(size, half, width) for size in sizes],
        scratch_shapes=[
            pltpu.VMEM((ROWS, rows, width), NARROW),
            pltpu.VMEM((rows, samples), NARROW),
        ],
        compiler_params=params(),
        cost_estimate=cost(2 * rows * records.size, 2 * (records.size + rows * half * width)),
    )(place, after, *tables, records.reshape(2, half, receivers, samples))


def inverse_dft(place, pieces, tables):
    half, width = pieces[0][0].shape[1:]
    receivers = width // 2
    samples = tables[0].shape[-1]
    spectra = [piece for group in pieces for piece in group]
    sizes = [piece.shape[0] for piece in spectra]
    rows = sum(sizes)

    def kernel(place_ref, *refs):
        table_refs = refs[:len(tables)]
        spectra_refs = refs[len(tables):len(tables) + len(spectra)]
        out_ref, turned, table = refs[len(tables) + len(spectra):]

        @pl.when(pl.program_id(0) == 0)
        def _():
            at = 0
            for table_ref, group in zip(table_refs, pieces):
                for part, piece in enumerate(group):
                    size = piece.shape[0]
                    which = (place_ref[0] ^ part) if len(group) > 1 else 0
                    table[at:at + size, :] = table_ref[which]
                    at += size

        at = 0
        for ref, size in zip(spectra_refs, sizes):
            turned[:, at:at + size, :] = jnp.swapaxes(ref[...], 0, 1)
            at += size
        for p in range(0, ROWS, BATCH):
            columns = [turned[p + q] for q in range(BATCH)]
            traces = lax.dot_general(
                jnp.concatenate(columns, axis=1), table[...], TN, preferred_element_type=WIDE
            ).astype(out_ref.dtype)
            for q in range(BATCH):
                out_ref[0, p + q] = traces[q * width:q * width + receivers]
                out_ref[1, p + q] = traces[q * width + receivers:(q + 1) * width]

    return pl.pallas_call(
        kernel,
        grid=(half // ROWS,),
        in_specs=[IN_SMEM]
        + [pl.BlockSpec(table.shape, lambda i: (0, 0, 0)) for table in tables]
        + [pl.BlockSpec((size, ROWS, width), lambda i: (0, i, 0)) for size in sizes],
        out_specs=pl.BlockSpec((2, ROWS, receivers, samples), lambda i: (0, i, 0, 0)),
        out_shape=shaped(2, half, receivers, samples),
        scratch_shapes=[
            pltpu.VMEM((ROWS, rows, width), NARROW),
            pltpu.VMEM((rows, samples), NARROW),
        ],
        compiler_params=params(),
        cost_estimate=cost(
            2 * rows * half * width * samples, 2 * half * width * (samples + rows)
        ),
    )(place, *tables, *spectra).reshape(2 * half, receivers, samples)


def swap_quarters(block):
    half = block.shape[0] // 2
    return jnp.concatenate(
        [
            jnp.concatenate([block[:half, :half], block[half:, :half]], axis=1),
            jnp.concatenate([block[:half, half:], block[half:, half:]], axis=1),
        ],
        axis=0,
    )


def left_half(rows, lanes):
    return lax.broadcasted_iota(jnp.int32, (rows, lanes), 1) < lanes // 2


def places(half):
    shape = (half, 2 * half)
    rows = lax.broadcasted_iota(jnp.int32, shape, 0)
    lanes = lax.broadcasted_iota(jnp.int32, shape, 1)
    left = lanes < half
    return rows, jnp.where(left, lanes, lanes - half), left


def pack_diagonals(real, imag):
    half = real.shape[0] // 2
    rows, lanes, left = places(half)
    packed, diagonals = [], []
    for block in (real, imag):
        lower = pltpu.roll(block[half:], half, 1)
        packed.append(jnp.where(left & (rows > lanes), lower, block[:half]))
        diagonals.append(jnp.where(rows == lanes, block[half:], 0.0))
    both = jnp.where(left, pltpu.roll(diagonals[0], half, 1), diagonals[1])
    both = jnp.sum(both, axis=0, keepdims=True)
    return packed[0], packed[1], jnp.broadcast_to(both, (ROWS, 2 * half))


def unpack_diagonal(packed, diagonals, c):
    half, size = packed.shape
    rows, lanes, left = places(half)
    mirrored = jnp.concatenate([packed, packed], axis=0).T
    diagonal = diagonals[:1]
    if c == 0:
        diagonal = pltpu.roll(jnp.broadcast_to(diagonal, (8, size)), half, 1)[:1]
    top = jnp.where(left & (rows > lanes), mirrored[:half], packed)
    last = jnp.where(rows > lanes, pltpu.roll(packed, half, 1), mirrored[:half])
    last = jnp.where(rows == lanes, diagonal, last)
    return jnp.concatenate([top, jnp.where(left, mirrored[half:], last)], axis=0)


def square(ref, *at):
    halves = ref[at] if at else ref[...]
    return halves.astype(WIDE).reshape(2 * halves.shape[-2], halves.shape[-1])


def dot(left, right):
    return jnp.dot(left, right, preferred_element_type=WIDE)


def series(real_k, imag_k, recip, first, out_block, tile):
    order = recip.shape[-1]
    panel = min(2 * tile, order)

    def scaled(real, imag):
        return real_k * real - imag_k * imag, real_k * imag + imag_k * real

    for start in range(0, order, panel):
        rows = pl.ds(start, panel)
        a, b = recip[0, rows, :], recip[1, rows, :]
        real, imag = scaled(
            dot(a, recip[0]) - dot(b, recip[1]), dot(a, recip[1]) + dot(b, recip[0])
        )
        first[0, rows, :] = real.astype(NARROW)
        first[1, rows, :] = imag.astype(NARROW)
    for start in range(0, order, panel):
        rows = pl.ds(start, panel)
        own = [first[c, rows, :].astype(WIDE) for c in range(2)]
        a, b = [(recip[c, rows, :].astype(WIDE) + own[c]).astype(NARROW) for c in range(2)]
        real, imag = scaled(
            dot(a, first[0]) - dot(b, first[1]), dot(a, first[1]) + dot(b, first[0])
        )
        real, imag = own[0] + real, own[1] + imag
        for row in range(0, panel, tile):
            for b in range(order // tile):
                at = (slice(row, row + tile), slice(b * tile, (b + 1) * tile))
                out_block(
                    (start + row) // tile, b, swap_quarters(real[at].astype(NARROW)), swap_quarters(imag[at].astype(NARROW))
                )


def far_rows(n, tile):
    pair = 2 * (n - 2) * tile
    return pair, pair + tile, pair + 2 * tile, pair + 2 * tile + ROWS


def other_rows(block, c, tile):
    at = (2 * (block - 2) + c) * tile
    return slice(at, at + tile)


def predict(place, coeff, moved, n, direct_in, direct_out, start, stop, after):
    freqs = stop - start
    half, tile = moved[0].shape[-2:]
    order = n * tile
    pair_at, diagonal_at, last_at, length = far_rows(n, tile)

    def kernel(place_ref, coeff_ref, after_ref, *refs):
        count = 1 if direct_in else n + 1
        moved_refs, refs = refs[:count], refs[count:]
        ahead = pl.program_id(0) == 0

        def far(i, rows):
            if i > 2:
                return moved_refs[i + 1][0, rows].astype(WIDE)
            one, other = (moved_refs[k][0, rows].astype(WIDE) for k in (2, 3))
            return jnp.where(ahead, one, other)

        count = 1 if direct_out else n
        out_refs, (recip, first) = refs[:count], refs[count:]
        me = place_ref[0]
        odd = me % 2 == 1

        def stacked(c, i, j):
            if direct_in:
                return square(moved_refs[0], pl.ds((j ^ me) * 2, 2), i, 0, c)
            if i < 2:
                return square(moved_refs[i], i ^ j, 0, c)
            return far(i, other_rows(i ^ j, c, tile))

        def mean(c, a, b):
            if direct_in or a < 2 or (a ^ b) >= 2:
                turned = stacked(c, b, a).astype(NARROW).T.astype(WIDE)
                return 0.5 * (stacked(c, a, b) + turned)
            if a == b:
                at = diagonal_at + c * half
                packed = far(a, slice(at, at + half))
                return unpack_diagonal(packed, far(a, slice(last_at, length)), c)
            here = far(a, slice(pair_at, pair_at + tile))
            there = far(b, slice(pair_at, pair_at + tile)).T
            return jnp.where(odd == (c == 0), here, there)

        for c in range(2):
            for a in range(n):
                for b in range(a + 1):
                    block = swap_quarters(mean(c, a, b).astype(NARROW))
                    rows, columns = slice(a * tile, (a + 1) * tile), slice(b * tile, (b + 1) * tile)
                    recip[c, rows, columns] = block.astype(NARROW)
                    if a != b:
                        recip[c, columns, rows] = block.astype(NARROW).T

        def out_block(a, b, real, imag):
            gap = a ^ b
            if not direct_out and a >= 2 and gap == 1:
                own = jnp.where(odd == (a % 2 == 0), imag, real).astype(NARROW)
                out_refs[a][0, pair_at:pair_at + tile] = own
                return
            if not direct_out and a >= 2 and gap == 0:
                at = diagonal_at
                for value in pack_diagonals(real.astype(WIDE), imag.astype(WIDE)):
                    out_refs[a][0, at:at + value.shape[0]] = value.astype(NARROW)
                    at += value.shape[0]
                return
            for c, value in enumerate((real, imag)):
                value = value.astype(NARROW)
                if not direct_out and a >= 2:
                    out_refs[a][0, other_rows(gap, c, tile)] = value
                    continue
                for h in range(2):
                    part = value[h * half:(h + 1) * half]
                    if direct_out:
                        out_refs[0][(b ^ me) * 2 + h, a, 0, c] = part
                    else:
                        out_refs[a][gap, 0, c, h] = part

        index = pl.program_id(0) + start
        series(coeff_ref[index, 0], coeff_ref[index, 1], recip, first, out_block, tile)

    whole = (2 * n, n, freqs, 2, half, tile)
    close = (n, freqs, 2, 2, half, tile)
    far = (freqs, length, tile)
    split_shapes = [shaped(*close)] * 2 + [shaped(*far)] * (n - 2)

    def specs(direct, first, split):
        if direct:
            block = (2 * n, n, 1, 2, half, tile)
            return [pl.BlockSpec(block, lambda i: (0, 0, i + first, 0, 0, 0))]
        close = pl.BlockSpec((n, 1, 2, 2, half, tile), lambda i: (0, i + first, 0, 0, 0, 0))
        far = pl.BlockSpec((1, length, tile), lambda i: (i + first, 0, 0))
        if not split:
            return [close] * 2 + [far] * (n - 2)
        one = pl.BlockSpec((1, length, tile), lambda i: (0, 0, 0))
        others = pl.BlockSpec((1, length, tile), lambda i: (jnp.maximum(i - 1, 0), 0, 0))
        return [close] * 2 + [one, others] + [far] * (n - 3)

    return pl.pallas_call(
        kernel,
        grid=(freqs,),
        in_specs=[IN_SMEM, IN_SMEM, UNREAD] + specs(direct_in, start, True),
        out_specs=specs(direct_out, 0, False),
        out_shape=[shaped(*whole)] if direct_out else split_shapes,
        scratch_shapes=[pltpu.VMEM((2, order, order), NARROW)] * 2,
        compiler_params=params(),
        cost_estimate=cost(16 * freqs * order**3, 16 * freqs * order**2),
    )(place, coeff / math.sqrt(order), after, *moved)


def gather_rows(place, moved, pairs, n, after):
    _, _, freqs, _, half, tile = moved.shape
    pair_at, diagonal_at, last_at, length = far_rows(n, tile)

    def kernel(place_ref, after_ref, moved_ref, pairs_ref, *out_refs):
        me = place_ref[0]
        mine = me % 2

        def halves(block):
            return pl.ds((me ^ block) * 2, 2)

        for d in range(2):
            for block in range(n):
                for f in range(freqs):
                    for c in range(2):
                        out_refs[d][block, f, c] = moved_ref[halves(block), me ^ d, f, c]
        for d in range(2, n):
            for f in range(freqs):
                out_ref, own = (out_refs[d + 1], f) if d > 2 or f else (out_refs[2], 0)
                own = f - 1 if d == 2 and f else own
                for block in range(2, n):
                    for c in range(2):
                        rows = moved_ref[halves(block), me ^ d, f, c].reshape(tile, tile)
                        out_ref[own, other_rows(block, c, tile)] = rows
                here = square(moved_ref, halves(1), me ^ d, f, mine)
                there = square(pairs_ref, (d ^ 1) - 2, slice(None), f)
                mean = (0.5 * (here + there.T)).astype(NARROW)
                out_ref[own, pair_at:pair_at + tile] = mean
                means = []
                for c in range(2):
                    block = square(moved_ref, halves(0), me ^ d, f, c)
                    means.append(0.5 * (block + block.T))
                at = diagonal_at
                for value in pack_diagonals(*means):
                    out_ref[own, at:at + value.shape[0]] = value.astype(NARROW)
                    at += value.shape[0]

    close, far = shaped(n, freqs, 2, 2, half, tile), shaped(freqs, length, tile)
    split = [shaped(count, length, tile) for count in (1, freqs - 1)]
    return pl.pallas_call(
        kernel,
        in_specs=[IN_SMEM, UNREAD] + [IN_VMEM] * 2,
        out_specs=[IN_VMEM] * (n + 1),
        out_shape=[close] * 2 + split + [far] * (n - 3),
        compiler_params=params(),
        cost_estimate=cost(0, 4 * moved.size),
    )(place, after, moved, pairs)


def scatter_rows(place, groups, pairs, n, after):
    tile = pairs.shape[-1]
    half = tile // 2
    counts = [rows[0].shape[1] for rows in groups]
    freqs = sum(counts)
    pair_at, diagonal_at, last_at, length = far_rows(n, tile)

    def kernel(place_ref, after_ref, *refs):
        pairs_ref, out_ref = refs[-2:]
        me = place_ref[0]
        mine = me % 2

        def put(block, d, f, c, value):
            value = value.astype(NARROW)
            at = (me ^ block) * 2
            out_ref[at, me ^ d, f, c] = value[:half]
            out_ref[at + 1, me ^ d, f, c] = value[half:]

        def put_all(row_refs, d, f, own):
            ref = row_refs[d]
            if d < 2:
                for block in range(n):
                    for c in range(2):
                        put(block, d, f, c, square(ref, block, own, c))
                return
            for block in range(2, n):
                for c in range(2):
                    put(block, d, f, c, ref[own, other_rows(block, c, tile)])
            put(1, d, f, mine, ref[own, pair_at:pair_at + tile])
            put(1, d, f, 1 - mine, pairs_ref[(d ^ 1) - 2, f].astype(WIDE).T)
            last = ref[own, last_at:length].astype(WIDE)
            for c in range(2):
                packed = ref[own, diagonal_at + c * half:diagonal_at + (c + 1) * half]
                put(0, d, f, c, unpack_diagonal(packed.astype(WIDE), last, c))

        f = 0
        for group, count in enumerate(counts):
            for own in range(count):
                for d in range(n):
                    put_all(refs[group * n:(group + 1) * n], d, f, own)
                f += 1

    arrays = [array for rows in groups for array in rows]
    return pl.pallas_call(
        kernel,
        in_specs=[IN_SMEM, UNREAD] + [IN_VMEM] * (len(arrays) + 1),
        out_specs=IN_VMEM,
        out_shape=shaped(2 * n, n, freqs, 2, half, tile),
        compiler_params=params(),
        cost_estimate=cost(0, 0),
    )(place, after, *arrays, pairs)


def apart(moved, start):
    shape = moved.shape
    n, freqs = shape[1], shape[2] - start

    def kernel(moved_ref, *out_refs):
        for part, ref in enumerate(out_refs):
            ref[...] = moved_ref[:, part, start:]

    return pl.pallas_call(
        kernel,
        in_specs=[IN_VMEM],
        out_specs=[IN_VMEM] * n,
        out_shape=[shaped(shape[0], freqs, *shape[3:])] * n,
        compiler_params=params(),
        cost_estimate=cost(0, 0),
    )(moved)


def gate(value, *after):
    return lax.optimization_barrier((value, *after))[0]


def chunk_sizes(per_group):
    return [per_group // 2, per_group - per_group // 2]


def swapped(value, gap):
    size = lax.axis_size("src")
    return lax.ppermute(value, "src", [(i, i ^ gap) for i in range(size)])


def spread(value):
    return lax.all_to_all(value, "rcv", split_axis=0, concat_axis=0, tiled=True)


def local_tiles(records, surface_operator):
    src_tiles, rcv_tiles, samples = records.shape
    freqs = surface_operator.shape[0]
    n = lax.axis_size("src")
    devices = 2 * n * n
    half = src_tiles // 2
    me, column = lax.axis_index("src"), lax.axis_index("rcv")
    place = me.astype(jnp.int32)[None]
    sizes = chunk_sizes(freqs // devices)
    starts = [devices * sum(sizes[:q]) for q in range(len(sizes))]

    forward, inverse = host_tables(freqs, samples)

    def rows_of(table, q):
        return table[starts[q]:starts[q] + devices * sizes[q]]

    def by_owner(table, q):
        rows = rows_of(table, q).reshape(2 * n, n, sizes[q] * 2, samples)
        return rows.swapaxes(0, 1).reshape(n, -1, samples)

    coeffs = []
    for q, size in enumerate(sizes):
        at = starts[q] + (column * n + me) * size
        coeffs.append(lax.dynamic_slice_in_dim(surface_operator, at, size, 0))

    def first_part(q):
        if q == 0:
            return jnp.asarray(by_owner(forward, 0))
        return jnp.asarray(rows_of(forward, q).reshape(1, -1, samples))

    def over_src(rows):
        return [rows[0]] + [swapped(rows[d], d) for d in range(1, n)]

    def pair_of(moved, q):
        theirs = 1 - me % 2
        pairs = []
        for d in range(2, n):
            at = ((me ^ 1) * 2, me ^ d, 0, theirs, 0, 0)
            pair = lax.dynamic_slice(moved, at, (2, 1, sizes[q], 1, half, src_tiles))
            pairs.append(pair.reshape(2, sizes[q], half, src_tiles))
        return swapped(jnp.stack(pairs), 1)

    def spread_chunk(spectrum, q):
        return spread(spectrum.reshape(2 * n, n, sizes[q], 2, half, src_tiles))

    def gather(moved, q, after):
        return gather_rows(place, moved, pair_of(moved, q), n, after)

    def pairs_of(groups):
        pair_at = far_rows(n, src_tiles)[0]
        return jnp.stack(
            [
                jnp.concatenate([rows[d][:, pair_at:pair_at + src_tiles] for rows in groups])
                for d in range(2, n)
            ]
        )

    def flat(moved):
        return moved.reshape(-1, half, src_tiles)

    *early, spectrum = forward_dft(place, records, [first_part(0), first_part(1)], place)
    early = over_src(early)
    moved1 = spread_chunk(spectrum, 1)
    sent1 = gather(moved1, 1, place)
    first, others = (swapped(rows, 2) for rows in sent1[2:4])
    rows1 = [sent1[0], swapped(sent1[1], 1), first, others]
    rows1 += [swapped(sent1[d + 1], d) for d in range(3, n)]
    parts = [part.reshape(2 * n, 1, sizes[0], 2, half, src_tiles) for part in early]
    joined = jnp.concatenate([gate(part, sent1[0]) for part in parts], axis=1)
    moved0 = spread(gate(joined, first))
    rest0 = predict(place, coeffs[0], [moved0], n, True, False, 1, sizes[0], sent1[0])
    sent0 = rest0[0]
    first0 = predict(place, coeffs[0], [moved0], n, True, False, 0, 1, sent0)
    sent0 = first0[0]
    first0 = over_src(first0)
    rest0 = over_src(rest0)
    back1 = predict(place, coeffs[1], rows1, n, False, True, 0, sizes[1], sent0)[0]
    moved = spread(gate(back1, *first0[1:]))
    first1 = over_src([moved[:, d, :1] for d in range(n)])
    rest1 = apart(moved, 1)
    sent1 = rest1[0]
    rest1 = over_src(rest1)
    pairs = swapped(pairs_of([first0, rest0]), 1)
    home0 = scatter_rows(place, [first0, rest0], pairs, n, sent1)
    home0 = spread(gate(home0, *first1[1:]))
    pieces = [[flat(home0)], [flat(x) for x in first1], [flat(x) for x in rest1]]
    last = by_owner(inverse, 1).reshape(n, 2 * n, sizes[1], 2, samples)
    tables = [
        jnp.asarray(rows_of(inverse, 0).reshape(1, -1, samples)),
        jnp.asarray(last[:, :, :1].reshape(n, -1, samples)),
        jnp.asarray(last[:, :, 1:].reshape(n, -1, samples)),
    ]
    return inverse_dft(place, pieces, tables)


def solution(mesh):
    placed = (P("src", "rcv", None), P())
    n_src, n_rcv = mesh.shape["src"], mesh.shape["rcv"]

    def local(records, surface_operator):
        src_tiles, rcv_tiles, _ = records.shape
        per_group = surface_operator.shape[0] // (n_src * n_rcv)
        square_tiles = n_rcv == 2 * n_src and src_tiles == 2 * rcv_tiles
        whole_lanes = src_tiles % 128 == 0 and n_src >= 4 and n_src & (n_src - 1) == 0
        if square_tiles and whole_lanes and per_group >= 4:
            return local_tiles(records, surface_operator)
        return local_general(records, surface_operator)

    return jax.shard_map(
        local, mesh=mesh, in_specs=placed, out_specs=P("src", "rcv", None), check_vma=False
    )
```

```python
import math

import jax
import jax.numpy as jnp
from jax import lax
from jax.sharding import PartitionSpec as P
from jax.experimental import pallas as pl
from jax.experimental.pallas import tpu as pltpu
import ml_dtypes
import numpy as np


def dft_tables(freqs, samples):
    freq_index = lax.broadcasted_iota(jnp.int32, (freqs, samples), 0)
    time_index = lax.broadcasted_iota(jnp.int32, (freqs, samples), 1)
    phase = (freq_index * time_index % samples).astype(jnp.float32)
    angle = phase * (2.0 * math.pi / samples)
    norming = 1.0 / math.sqrt(samples)
    cosine = jnp.cos(angle) * norming
    sine = jnp.sin(angle) * norming
    weights = jnp.where(freq_index == 0, 1.0, 2.0).astype(jnp.float32)
    forward = jnp.stack([cosine, -sine], axis=1).reshape(2 * freqs, samples)
    inverse = jnp.stack([weights * cosine, -weights * sine], axis=1).reshape(2 * freqs, samples)
    return (forward.astype(jnp.bfloat16), inverse.astype(jnp.bfloat16))


def batch_product(left, right):

    def mult(first_op, second_op):
        return jnp.einsum("nij,njk->nik", first_op, second_op, preferred_element_type=jnp.float32)

    real_part = mult(left[:, 0], right[:, 0]) - mult(left[:, 1], right[:, 1])
    imag_part = mult(left[:, 0], right[:, 1]) + mult(left[:, 1], right[:, 0])
    return (real_part, imag_part)


def predict_block(blocks, coeff):
    order = blocks.shape[2]
    recip = (
        0.5 * (blocks.astype(jnp.float32) + jnp.swapaxes(blocks, 2, 3).astype(jnp.float32))
    ).astype(jnp.bfloat16)
    factor = coeff / math.sqrt(order)
    real_k = factor[:, 0][:, None, None]
    imag_k = factor[:, 1][:, None, None]

    def scaled(product):
        return jnp.stack(
            [real_k * product[0] - imag_k * product[1], real_k * product[1] + imag_k * product[0]],
            axis=1,
        )

    first = scaled(batch_product(recip, recip)).astype(jnp.bfloat16)
    second = scaled(batch_product(recip, first)).astype(jnp.bfloat16)
    third = scaled(batch_product(recip, second))
    return (first.astype(jnp.float32) + second.astype(jnp.float32) + third).astype(jnp.bfloat16)


def local_general(records, surface_operator):
    src_tiles, rcv_tiles, samples = records.shape
    freqs = surface_operator.shape[0]
    n_src = lax.axis_size("src")
    n_rcv = lax.axis_size("rcv")
    per_group = freqs // (n_src * n_rcv)
    columns = src_tiles * rcv_tiles
    whole_src = n_src * src_tiles
    whole_rcv = n_rcv * rcv_tiles
    forward, inverse = dft_tables(freqs, samples)
    flat_traces = records.reshape(columns, samples)
    spectrum = jnp.einsum(
        "kt,nt->kn", forward, flat_traces, preferred_element_type=jnp.float32
    ).astype(jnp.bfloat16)
    group_index = lax.axis_index("src") * n_rcv + lax.axis_index("rcv")
    coeff = lax.dynamic_slice_in_dim(surface_operator, group_index * per_group, per_group, 0)
    moved = lax.all_to_all(
        spectrum.reshape(freqs, 2, 1, columns),
        ("src", "rcv"),
        split_axis=0,
        concat_axis=2,
        tiled=True,
    )
    blocks = moved.reshape(per_group, 2, n_src, n_rcv, src_tiles, rcv_tiles)
    blocks = blocks.transpose(0, 1, 2, 4, 3, 5).reshape(per_group, 2, whole_src, whole_rcv)
    predicted = predict_block(blocks, coeff)
    outgoing = predicted.reshape(per_group, 2, n_src, src_tiles, n_rcv, rcv_tiles).transpose(
        0, 1, 2, 4, 3, 5
    )
    returned = lax.all_to_all(
        outgoing.reshape(1, per_group, 2, n_src * n_rcv, columns),
        ("src", "rcv"),
        split_axis=3,
        concat_axis=0,
        tiled=True,
    )
    returned = returned.reshape(2 * freqs, columns)
    result = jnp.einsum("kn,kt->nt", returned, inverse, preferred_element_type=jnp.float32)
    return result.astype(jnp.bfloat16).reshape(src_tiles, rcv_tiles, samples)


NT = (((1,), (1,)), ((), ()))
TN = (((0,), (0,)), ((), ()))
VMEM_LIMIT = 56 * 2**20
ROWS = 16
BATCH = 8
WIDE = jnp.float32
NARROW = jnp.bfloat16
IN_VMEM = pl.BlockSpec(memory_space=pltpu.VMEM)
IN_SMEM = pl.BlockSpec(memory_space=pltpu.SMEM)
UNREAD = pl.BlockSpec(memory_space=pl.ANY)


def host_tables(freqs, samples):
    f = np.arange(freqs)[:, None]
    t = np.arange(samples)[None, :]
    angle = (f * t % samples) * (2.0 * math.pi / samples)
    norming = 1.0 / math.sqrt(samples)
    cosine = np.cos(angle) * norming
    sine = np.sin(angle) * norming
    weights = np.where(f == 0, 1.0, 2.0)
    forward = np.stack([cosine, -sine], axis=1)
    inverse = np.stack([weights * cosine, -weights * sine], axis=1)
    return [x.astype(np.float32).astype(ml_dtypes.bfloat16) for x in (forward, inverse)]


def params():
    return pltpu.CompilerParams(vmem_limit_bytes=VMEM_LIMIT)


def cost(flops, moved):
    return pl.CostEstimate(flops=0, bytes_accessed=0, transcendentals=0)


def shaped(*shape):
    return jax.ShapeDtypeStruct(shape, NARROW)


def forward_dft(place, records, tables, after):
    sources, receivers, samples = records.shape
    half = sources // 2
    width = 2 * receivers
    sizes = [table.shape[1] for table in tables for _ in range(table.shape[0])]
    rows = sum(sizes)

    def kernel(place_ref, after_ref, *refs):
        table_refs, records_ref = refs[:len(tables)], refs[len(tables)]
        out_refs, (turned, table) = refs[len(tables) + 1:-2], refs[-2:]

        @pl.when(pl.program_id(0) == 0)
        def _():
            at = 0
            for ref in table_refs:
                parts, size, _ = ref.shape
                for part in range(parts):
                    which = (place_ref[0] ^ part) if parts > 1 else 0
                    table[at:at + size, :] = ref[which]
                    at += size

        for p in range(0, ROWS, 2):
            traces = jnp.concatenate(
                [records_ref[s, p + d] for d in range(2) for s in range(2)], axis=0
            )
            found = lax.dot_general(table[...], traces, NT, preferred_element_type=WIDE)
            found = found.astype(NARROW)
            turned[p] = found[:, :width]
            turned[p + 1] = found[:, width:]
        at = 0
        for out_ref, size in zip(out_refs, sizes):
            out_ref[...] = jnp.swapaxes(turned[:, at:at + size, :], 0, 1)
            at += size

    return pl.pallas_call(
        kernel,
        grid=(half // ROWS,),
        in_specs=[IN_SMEM, UNREAD]
        + [pl.BlockSpec(table.shape, lambda i: (0, 0, 0)) for table in tables]
        + [pl.BlockSpec((2, ROWS, receivers, samples), lambda i: (0, i, 0, 0))],
        out_specs=[pl.BlockSpec((size, ROWS, width), lambda i: (0, i, 0)) for size in sizes],
        out_shape=[shaped(size, half, width) for size in sizes],
        scratch_shapes=[
            pltpu.VMEM((ROWS, rows, width), NARROW),
            pltpu.VMEM((rows, samples), NARROW),
        ],
        compiler_params=params(),
        cost_estimate=cost(2 * rows * records.size, 2 * (records.size + rows * half * width)),
    )(place, after, *tables, records.reshape(2, half, receivers, samples))


def inverse_dft(place, pieces, tables):
    half, width = pieces[0][0].shape[1:]
    receivers = width // 2
    samples = tables[0].shape[-1]
    spectra = [piece for group in pieces for piece in group]
    sizes = [piece.shape[0] for piece in spectra]
    rows = sum(sizes)

    def kernel(place_ref, *refs):
        table_refs = refs[:len(tables)]
        spectra_refs = refs[len(tables):len(tables) + len(spectra)]
        out_ref, turned, table = refs[len(tables) + len(spectra):]

        @pl.when(pl.program_id(0) == 0)
        def _():
            at = 0
            for table_ref, group in zip(table_refs, pieces):
                for part, piece in enumerate(group):
                    size = piece.shape[0]
                    which = (place_ref[0] ^ part) if len(group) > 1 else 0
                    table[at:at + size, :] = table_ref[which]
                    at += size

        at = 0
        for ref, size in zip(spectra_refs, sizes):
            turned[:, at:at + size, :] = jnp.swapaxes(ref[...], 0, 1)
            at += size
        for p in range(0, ROWS, BATCH):
            columns = [turned[p + q] for q in range(BATCH)]
            traces = lax.dot_general(
                jnp.concatenate(columns, axis=1), table[...], TN, preferred_element_type=WIDE
            ).astype(out_ref.dtype)
            for q in range(BATCH):
                out_ref[0, p + q] = traces[q * width:q * width + receivers]
                out_ref[1, p + q] = traces[q * width + receivers:(q + 1) * width]

    return pl.pallas_call(
        kernel,
        grid=(half // ROWS,),
        in_specs=[IN_SMEM]
        + [pl.BlockSpec(table.shape, lambda i: (0, 0, 0)) for table in tables]
        + [pl.BlockSpec((size, ROWS, width), lambda i: (0, i, 0)) for size in sizes],
        out_specs=pl.BlockSpec((2, ROWS, receivers, samples), lambda i: (0, i, 0, 0)),
        out_shape=shaped(2, half, receivers, samples),
        scratch_shapes=[
            pltpu.VMEM((ROWS, rows, width), NARROW),
            pltpu.VMEM((rows, samples), NARROW),
        ],
        compiler_params=params(),
        cost_estimate=cost(
            2 * rows * half * width * samples, 2 * half * width * (samples + rows)
        ),
    )(place, *tables, *spectra).reshape(2 * half, receivers, samples)


def swap_quarters(block):
    half = block.shape[0] // 2
    return jnp.concatenate(
        [
            jnp.concatenate([block[:half, :half], block[half:, :half]], axis=1),
            jnp.concatenate([block[:half, half:], block[half:, half:]], axis=1),
        ],
        axis=0,
    )


def left_half(rows, lanes):
    return lax.broadcasted_iota(jnp.int32, (rows, lanes), 1) < lanes // 2


def places(half):
    shape = (half, 2 * half)
    rows = lax.broadcasted_iota(jnp.int32, shape, 0)
    lanes = lax.broadcasted_iota(jnp.int32, shape, 1)
    left = lanes < half
    return rows, jnp.where(left, lanes, lanes - half), left


def pack_diagonals(real, imag):
    half = real.shape[0] // 2
    rows, lanes, left = places(half)
    packed, diagonals = [], []
    for block in (real, imag):
        lower = pltpu.roll(block[half:], half, 1)
        packed.append(jnp.where(left & (rows > lanes), lower, block[:half]))
        diagonals.append(jnp.where(rows == lanes, block[half:], 0.0))
    both = jnp.where(left, pltpu.roll(diagonals[0], half, 1), diagonals[1])
    both = jnp.sum(both, axis=0, keepdims=True)
    return packed[0], packed[1], jnp.broadcast_to(both, (ROWS, 2 * half))


def unpack_diagonal(packed, diagonals, c):
    half, size = packed.shape
    rows, lanes, left = places(half)
    mirrored = jnp.concatenate([packed, packed], axis=0).T
    diagonal = diagonals[:1]
    if c == 0:
        diagonal = pltpu.roll(jnp.broadcast_to(diagonal, (8, size)), half, 1)[:1]
    top = jnp.where(left & (rows > lanes), mirrored[:half], packed)
    last = jnp.where(rows > lanes, pltpu.roll(packed, half, 1), mirrored[:half])
    last = jnp.where(rows == lanes, diagonal, last)
    return jnp.concatenate([top, jnp.where(left, mirrored[half:], last)], axis=0)


def square(ref, *at):
    halves = ref[at] if at else ref[...]
    return halves.astype(WIDE).reshape(2 * halves.shape[-2], halves.shape[-1])


def dot(left, right):
    return jnp.dot(left, right, preferred_element_type=WIDE)


def series(real_k, imag_k, recip, first, out_block, tile):
    order = recip.shape[-1]
    panel = min(2 * tile, order)

    def scaled(real, imag):
        return real_k * real - imag_k * imag, real_k * imag + imag_k * real

    for start in range(0, order, panel):
        rows = pl.ds(start, panel)
        a, b = recip[0, rows, :], recip[1, rows, :]
        real, imag = scaled(
            dot(a, recip[0]) - dot(b, recip[1]), dot(a, recip[1]) + dot(b, recip[0])
        )
        first[0, rows, :] = real.astype(NARROW)
        first[1, rows, :] = imag.astype(NARROW)
    for start in range(0, order, panel):
        rows = pl.ds(start, panel)
        own = [first[c, rows, :].astype(WIDE) for c in range(2)]
        a, b = [(recip[c, rows, :].astype(WIDE) + own[c]).astype(NARROW) for c in range(2)]
        real, imag = scaled(
            dot(a, first[0]) - dot(b, first[1]), dot(a, first[1]) + dot(b, first[0])
        )
        real, imag = own[0] + real, own[1] + imag
        for row in range(0, panel, tile):
            for b in range(order // tile):
                at = (slice(row, row + tile), slice(b * tile, (b + 1) * tile))
                out_block(
                    (start + row) // tile, b, swap_quarters(real[at].astype(NARROW)), swap_quarters(imag[at].astype(NARROW))
                )


def far_rows(n, tile):
    pair = 2 * (n - 2) * tile
    return pair, pair + tile, pair + 2 * tile, pair + 2 * tile + ROWS


def other_rows(block, c, tile):
    at = (2 * (block - 2) + c) * tile
    return slice(at, at + tile)


def predict(place, coeff, moved, n, direct_in, direct_out, start, stop, after):
    freqs = stop - start
    half, tile = moved[0].shape[-2:]
    order = n * tile
    pair_at, diagonal_at, last_at, length = far_rows(n, tile)

    def kernel(place_ref, coeff_ref, after_ref, *refs):
        count = 1 if direct_in else n + 1
        moved_refs, refs = refs[:count], refs[count:]
        ahead = pl.program_id(0) == 0

        def far(i, rows):
            if i > 2:
                return moved_refs[i + 1][0, rows].astype(WIDE)
            one, other = (moved_refs[k][0, rows].astype(WIDE) for k in (2, 3))
            return jnp.where(ahead, one, other)

        count = 1 if direct_out else n
        out_refs, (recip, first) = refs[:count], refs[count:]
        me = place_ref[0]
        odd = me % 2 == 1

        def stacked(c, i, j):
            if direct_in:
                return square(moved_refs[0], pl.ds((j ^ me) * 2, 2), i, 0, c)
            if i < 2:
                return square(moved_refs[i], i ^ j, 0, c)
            return far(i, other_rows(i ^ j, c, tile))

        def mean(c, a, b):
            if direct_in or a < 2 or (a ^ b) >= 2:
                turned = stacked(c, b, a).astype(NARROW).T.astype(WIDE)
                return 0.5 * (stacked(c, a, b) + turned)
            if a == b:
                at = diagonal_at + c * half
                packed = far(a, slice(at, at + half))
                return unpack_diagonal(packed, far(a, slice(last_at, length)), c)
            here = far(a, slice(pair_at, pair_at + tile))
            there = far(b, slice(pair_at, pair_at + tile)).T
            return jnp.where(odd == (c == 0), here, there)

        for c in range(2):
            for a in range(n):
                for b in range(a + 1):
                    block = swap_quarters(mean(c, a, b).astype(NARROW))
                    rows, columns = slice(a * tile, (a + 1) * tile), slice(b * tile, (b + 1) * tile)
                    recip[c, rows, columns] = block.astype(NARROW)
                    if a != b:
                        recip[c, columns, rows] = block.astype(NARROW).T

        def out_block(a, b, real, imag):
            gap = a ^ b
            if not direct_out and a >= 2 and gap == 1:
                own = jnp.where(odd == (a % 2 == 0), imag, real).astype(NARROW)
                out_refs[a][0, pair_at:pair_at + tile] = own
                return
            if not direct_out and a >= 2 and gap == 0:
                at = diagonal_at
                for value in pack_diagonals(real.astype(WIDE), imag.astype(WIDE)):
                    out_refs[a][0, at:at + value.shape[0]] = value.astype(NARROW)
                    at += value.shape[0]
                return
            for c, value in enumerate((real, imag)):
                value = value.astype(NARROW)
                if not direct_out and a >= 2:
                    out_refs[a][0, other_rows(gap, c, tile)] = value
                    continue
                for h in range(2):
                    part = value[h * half:(h + 1) * half]
                    if direct_out:
                        out_refs[0][(b ^ me) * 2 + h, a, 0, c] = part
                    else:
                        out_refs[a][gap, 0, c, h] = part

        index = pl.program_id(0) + start
        series(coeff_ref[index, 0], coeff_ref[index, 1], recip, first, out_block, tile)

    whole = (2 * n, n, freqs, 2, half, tile)
    close = (n, freqs, 2, 2, half, tile)
    far = (freqs, length, tile)
    split_shapes = [shaped(*close)] * 2 + [shaped(*far)] * (n - 2)

    def specs(direct, first, split):
        if direct:
            block = (2 * n, n, 1, 2, half, tile)
            return [pl.BlockSpec(block, lambda i: (0, 0, i + first, 0, 0, 0))]
        close = pl.BlockSpec((n, 1, 2, 2, half, tile), lambda i: (0, i + first, 0, 0, 0, 0))
        far = pl.BlockSpec((1, length, tile), lambda i: (i + first, 0, 0))
        if not split:
            return [close] * 2 + [far] * (n - 2)
        one = pl.BlockSpec((1, length, tile), lambda i: (0, 0, 0))
        others = pl.BlockSpec((1, length, tile), lambda i: (jnp.maximum(i - 1, 0), 0, 0))
        return [close] * 2 + [one, others] + [far] * (n - 3)

    return pl.pallas_call(
        kernel,
        grid=(freqs,),
        in_specs=[IN_SMEM, IN_SMEM, UNREAD] + specs(direct_in, start, True),
        out_specs=specs(direct_out, 0, False),
        out_shape=[shaped(*whole)] if direct_out else split_shapes,
        scratch_shapes=[pltpu.VMEM((2, order, order), NARROW)] * 2,
        compiler_params=params(),
        cost_estimate=cost(16 * freqs * order**3, 16 * freqs * order**2),
    )(place, coeff / math.sqrt(order), after, *moved)


def gather_rows(place, moved, pairs, n, after):
    _, _, freqs, _, half, tile = moved.shape
    pair_at, diagonal_at, last_at, length = far_rows(n, tile)

    def kernel(place_ref, after_ref, moved_ref, pairs_ref, *out_refs):
        me = place_ref[0]
        mine = me % 2

        def halves(block):
            return pl.ds((me ^ block) * 2, 2)

        for d in range(2):
            for block in range(n):
                for f in range(freqs):
                    for c in range(2):
                        out_refs[d][block, f, c] = moved_ref[halves(block), me ^ d, f, c]
        for d in range(2, n):
            for f in range(freqs):
                out_ref, own = (out_refs[d + 1], f) if d > 2 or f else (out_refs[2], 0)
                own = f - 1 if d == 2 and f else own
                for block in range(2, n):
                    for c in range(2):
                        rows = moved_ref[halves(block), me ^ d, f, c].reshape(tile, tile)
                        out_ref[own, other_rows(block, c, tile)] = rows
                here = square(moved_ref, halves(1), me ^ d, f, mine)
                there = square(pairs_ref, (d ^ 1) - 2, slice(None), f)
                mean = (0.5 * (here + there.T)).astype(NARROW)
                out_ref[own, pair_at:pair_at + tile] = mean
                means = []
                for c in range(2):
                    block = square(moved_ref, halves(0), me ^ d, f, c)
                    means.append(0.5 * (block + block.T))
                at = diagonal_at
                for value in pack_diagonals(*means):
                    out_ref[own, at:at + value.shape[0]] = value.astype(NARROW)
                    at += value.shape[0]

    close, far = shaped(n, freqs, 2, 2, half, tile), shaped(freqs, length, tile)
    split = [shaped(count, length, tile) for count in (1, freqs - 1)]
    return pl.pallas_call(
        kernel,
        in_specs=[IN_SMEM, UNREAD] + [IN_VMEM] * 2,
        out_specs=[IN_VMEM] * (n + 1),
        out_shape=[close] * 2 + split + [far] * (n - 3),
        compiler_params=params(),
        cost_estimate=cost(0, 4 * moved.size),
    )(place, after, moved, pairs)


def scatter_rows(place, groups, pairs, n, after):
    tile = pairs.shape[-1]
    half = tile // 2
    counts = [rows[0].shape[1] for rows in groups]
    freqs = sum(counts)
    pair_at, diagonal_at, last_at, length = far_rows(n, tile)

    def kernel(place_ref, after_ref, *refs):
        pairs_ref, out_ref = refs[-2:]
        me = place_ref[0]
        mine = me % 2

        def put(block, d, f, c, value):
            value = value.astype(NARROW)
            at = (me ^ block) * 2
            out_ref[at, me ^ d, f, c] = value[:half]
            out_ref[at + 1, me ^ d, f, c] = value[half:]

        def put_all(row_refs, d, f, own):
            ref = row_refs[d]
            if d < 2:
                for block in range(n):
                    for c in range(2):
                        put(block, d, f, c, square(ref, block, own, c))
                return
            for block in range(2, n):
                for c in range(2):
                    put(block, d, f, c, ref[own, other_rows(block, c, tile)])
            put(1, d, f, mine, ref[own, pair_at:pair_at + tile])
            put(1, d, f, 1 - mine, pairs_ref[(d ^ 1) - 2, f].astype(WIDE).T)
            last = ref[own, last_at:length].astype(WIDE)
            for c in range(2):
                packed = ref[own, diagonal_at + c * half:diagonal_at + (c + 1) * half]
                put(0, d, f, c, unpack_diagonal(packed.astype(WIDE), last, c))

        f = 0
        for group, count in enumerate(counts):
            for own in range(count):
                for d in range(n):
                    put_all(refs[group * n:(group + 1) * n], d, f, own)
                f += 1

    arrays = [array for rows in groups for array in rows]
    return pl.pallas_call(
        kernel,
        in_specs=[IN_SMEM, UNREAD] + [IN_VMEM] * (len(arrays) + 1),
        out_specs=IN_VMEM,
        out_shape=shaped(2 * n, n, freqs, 2, half, tile),
        compiler_params=params(),
        cost_estimate=cost(0, 0),
    )(place, after, *arrays, pairs)


def apart(moved, start):
    shape = moved.shape
    n, freqs = shape[1], shape[2] - start

    def kernel(moved_ref, *out_refs):
        for part, ref in enumerate(out_refs):
            ref[...] = moved_ref[:, part, start:]

    return pl.pallas_call(
        kernel,
        in_specs=[IN_VMEM],
        out_specs=[IN_VMEM] * n,
        out_shape=[shaped(shape[0], freqs, *shape[3:])] * n,
        compiler_params=params(),
        cost_estimate=cost(0, 0),
    )(moved)


def gate(value, *after):
    return lax.optimization_barrier((value, *after))[0]


def chunk_sizes(per_group):
    return [per_group // 2, per_group - per_group // 2]


def swapped(value, gap):
    size = lax.axis_size("src")
    return lax.ppermute(value, "src", [(i, i ^ gap) for i in range(size)])


def spread(value):
    return lax.all_to_all(value, "rcv", split_axis=0, concat_axis=0, tiled=True)


def local_tiles(records, surface_operator):
    src_tiles, rcv_tiles, samples = records.shape
    freqs = surface_operator.shape[0]
    n = lax.axis_size("src")
    devices = 2 * n * n
    half = src_tiles // 2
    me, column = lax.axis_index("src"), lax.axis_index("rcv")
    place = me.astype(jnp.int32)[None]
    sizes = chunk_sizes(freqs // devices)
    starts = [devices * sum(sizes[:q]) for q in range(len(sizes))]

    forward, inverse = host_tables(freqs, samples)

    def rows_of(table, q):
        return table[starts[q]:starts[q] + devices * sizes[q]]

    def by_owner(table, q):
        rows = rows_of(table, q).reshape(2 * n, n, sizes[q] * 2, samples)
        return rows.swapaxes(0, 1).reshape(n, -1, samples)

    coeffs = []
    for q, size in enumerate(sizes):
        at = starts[q] + (column * n + me) * size
        coeffs.append(lax.dynamic_slice_in_dim(surface_operator, at, size, 0))

    def first_part(q):
        if q == 0:
            return jnp.asarray(by_owner(forward, 0))
        return jnp.asarray(rows_of(forward, q).reshape(1, -1, samples))

    def over_src(rows):
        return [rows[0]] + [swapped(rows[d], d) for d in range(1, n)]

    def pair_of(moved, q):
        theirs = 1 - me % 2
        pairs = []
        for d in range(2, n):
            at = ((me ^ 1) * 2, me ^ d, 0, theirs, 0, 0)
            pair = lax.dynamic_slice(moved, at, (2, 1, sizes[q], 1, half, src_tiles))
            pairs.append(pair.reshape(2, sizes[q], half, src_tiles))
        return swapped(jnp.stack(pairs), 1)

    def spread_chunk(spectrum, q):
        return spread(spectrum.reshape(2 * n, n, sizes[q], 2, half, src_tiles))

    def gather(moved, q, after):
        return gather_rows(place, moved, pair_of(moved, q), n, after)

    def pairs_of(groups):
        pair_at = far_rows(n, src_tiles)[0]
        return jnp.stack(
            [
                jnp.concatenate([rows[d][:, pair_at:pair_at + src_tiles] for rows in groups])
                for d in range(2, n)
            ]
        )

    def flat(moved):
        return moved.reshape(-1, half, src_tiles)

    *early, spectrum = forward_dft(place, records, [first_part(0), first_part(1)], place)
    early = over_src(early)
    moved1 = spread_chunk(spectrum, 1)
    sent1 = gather(moved1, 1, place)
    first, others = (swapped(rows, 2) for rows in sent1[2:4])
    rows1 = [sent1[0], swapped(sent1[1], 1), first, others]
    rows1 += [swapped(sent1[d + 1], d) for d in range(3, n)]
    parts = [part.reshape(2 * n, 1, sizes[0], 2, half, src_tiles) for part in early]
    joined = jnp.concatenate([gate(part, sent1[0]) for part in parts], axis=1)
    moved0 = spread(gate(joined, first))
    rest0 = predict(place, coeffs[0], [moved0], n, True, False, 1, sizes[0], sent1[0])
    sent0 = rest0[0]
    first0 = predict(place, coeffs[0], [moved0], n, True, False, 0, 1, sent0)
    sent0 = first0[0]
    first0 = over_src(first0)
    rest0 = over_src(rest0)
    back1 = predict(place, coeffs[1], rows1, n, False, True, 0, sizes[1], sent0)[0]
    moved = spread(gate(back1, *first0[1:]))
    first1 = over_src([moved[:, d, :1] for d in range(n)])
    rest1 = apart(moved, 1)
    sent1 = rest1[0]
    rest1 = over_src(rest1)
    pairs = swapped(pairs_of([first0, rest0]), 1)
    home0 = scatter_rows(place, [first0, rest0], pairs, n, sent1)
    home0 = spread(gate(home0, *first1[1:]))
    pieces = [[flat(home0)], [flat(x) for x in first1], [flat(x) for x in rest1]]
    last = by_owner(inverse, 1).reshape(n, 2 * n, sizes[1], 2, samples)
    tables = [
        jnp.asarray(rows_of(inverse, 0).reshape(1, -1, samples)),
        jnp.asarray(last[:, :, :1].reshape(n, -1, samples)),
        jnp.asarray(last[:, :, 1:].reshape(n, -1, samples)),
    ]
    return inverse_dft(place, pieces, tables)


def solution(mesh):
    placed = (P("src", "rcv", None), P())
    n_src, n_rcv = mesh.shape["src"], mesh.shape["rcv"]

    def local(records, surface_operator):
        src_tiles, rcv_tiles, _ = records.shape
        per_group = surface_operator.shape[0] // (n_src * n_rcv)
        square_tiles = n_rcv == 2 * n_src and src_tiles == 2 * rcv_tiles
        whole_lanes = src_tiles % 128 == 0 and n_src >= 4 and n_src & (n_src - 1) == 0
        if square_tiles and whole_lanes and per_group >= 4:
            return local_tiles(records, surface_operator)
        return local_general(records, surface_operator)

    return jax.shard_map(
        local, mesh=mesh, in_specs=placed, out_specs=P("src", "rcv", None), check_vma=False
    )
```
